256 devices in a mesh: head: 8 (over z_lo, core), depth: 32 (over x, y, z_hi).
Axes of the slice: x: 4, y: 4, z: 8 (z_hi: 2, z_lo: 4; z = z_hi * 4 + z_lo), core: 2. Of those that a mesh axis runs over, the one named last changes fastest.
Arguments:
- tokens: bfloat16 [128, 1280, 768], P('depth', 'head'), may hold values from -6 to 6
- ln_gain: float32 [768], replicated, may hold values from 0.1 to 1.9
- w_qkv: bfloat16 [768, 3, 512], replicated, may hold values from -0.21875 to 0.21875
- w_out: bfloat16 [512, 768], replicated, may hold values from -2.390625 to 2.390625
Outputs:
- mixed: float32 [128, 1280, 768], P('depth', 'head')
The draws below stay inside these ranges and needn't reach their ends.
All inputs are finite; a program needn't handle non-finite values.
Results may differ from the reference program's by a relative error of at most 0.0095.
Values may be sent and summed in bfloat16 or wider, within the bound.
No kernel may reach another device: no remote copies, remote signals or barrier semaphores. Data moves between devices by JAX's collectives and lax.ppermute only.
A program may use at most 64 MiB of HBM per device.

```python
import math
import jax
import jax.numpy as jnp
from jax import lax

D = 768
HEADS = 8
HEAD_DIM = 64
ROWS = 128
RES = 1280
INNER = 512


def block_scale(rng, extent, shards, low, high):
    def one(position, blocks):
        heights = jax.random.uniform(jax.random.fold_in(jax.random.fold_in(rng, 6), position), (blocks,), jnp.float32, low / len(shards), high / len(shards))
        return jnp.repeat(jnp.exp(heights), extent[position] // blocks).reshape((-1,) + (1,) * (len(extent) - position - 1))

    level = one(*shards[0])
    for cut in shards[1:]:
        level = level * one(*cut)
    return level


def noise(rng, shape, spread, limit, shards=(), dtype=jnp.bfloat16):
    level = block_scale(rng, shape, shards, -0.22, 0.18) if shards else 1.0
    values = jax.random.normal(rng, shape, jnp.float32) * spread * level
    return jnp.minimum(jnp.maximum(values, -limit), limit).astype(dtype)


def setup_inputs(seed: int = 0) -> dict:
    key_of = jax.random.split(jax.random.key(seed), 5)
    return {
        "tokens": noise(key_of[0], (ROWS, RES, D), 1.0, 6.0, ((0, 32), (1, 8))),
        "ln_gain": jnp.clip(1.0 + 0.18 * jax.random.normal(key_of[1], (D,), jnp.float32), 0.1, 1.9),
        "w_qkv": noise(key_of[2], (D, 3, INNER), D ** -0.5, 0.21875),
        "w_out": noise(key_of[3], (INNER, D), 0.4, 2.390625),
    }


def reference(tokens, ln_gain, w_qkv, w_out):
    x = tokens.astype(jnp.float32)
    mean = lax.optimization_barrier(jnp.mean(x, axis=-1, keepdims=True))
    var = lax.optimization_barrier(jnp.mean((x - mean) ** 2, axis=-1, keepdims=True))
    normed = ((x - mean) / jnp.sqrt(var + 1e-05) * ln_gain).astype(jnp.bfloat16)
    qkv = jnp.einsum('rld,dcf->rlcf', normed.astype(jnp.float32), w_qkv.astype(jnp.float32)).astype(jnp.bfloat16)
    shape = (ROWS, RES, HEADS, HEAD_DIM)
    query = qkv[:, :, 0].reshape(shape).astype(jnp.float32)
    keys = qkv[:, :, 1].reshape(shape).astype(jnp.float32)
    values = qkv[:, :, 2].reshape(shape).astype(jnp.float32)
    logits = jnp.einsum('rihe,rjhe->ihj', query, keys) * (1.0 / math.sqrt(HEAD_DIM * ROWS))
    expo = jnp.exp(logits)
    probs = (expo / lax.optimization_barrier(jnp.sum(expo, axis=-1, keepdims=True))).astype(jnp.bfloat16)
    context = jnp.einsum('ihj,rjhe->rihe', probs.astype(jnp.float32), values).astype(jnp.bfloat16)
    context = context.reshape(ROWS, RES, INNER)
    mixed = jnp.einsum('rlf,fd->rld', context.astype(jnp.float32), w_out.astype(jnp.float32))
    return mixed.astype(jnp.float32)
```

```python
import functools
import math

import jax
import jax.numpy as jnp
from jax import lax
from jax.experimental import pallas as pl
from jax.experimental.pallas import tpu as pltpu
from jax.sharding import Mesh
from jax.sharding import PartitionSpec as P

HEAD_DIM = 64
Z, CORE, X, Y, W = 4, 2, 4, 4, 2
RING = Z * W
PLANE = X * Y
BF = jnp.bfloat16
F32 = jnp.float32
VMEM = pl.BlockSpec(memory_space=pltpu.VMEM)
SMEM = pl.BlockSpec(memory_space=pltpu.SMEM)
PARAMS = pltpu.CompilerParams(vmem_limit_bytes=48 * 1024 * 1024)


def place(index):
    return (index % W) * Z + index // W


def index_of(position):
    return (position % Z) * W + position // Z


def head_at(position):
    pos = lax.rem(position, RING)
    return lax.rem(pos, Z) * W + lax.div(pos, Z)


def project_kernel(pos_ref, x_ref, gain_ref, w_ref, *refs):
    outs, (normed, mine) = refs[:-2], refs[-2:]
    seqs, length, width = x_ref.shape
    inner = w_ref.shape[2]
    heads = inner // HEAD_DIM
    for r in range(seqs):
        x = x_ref[r].astype(F32)
        mean = jnp.mean(x, axis=-1, keepdims=True)
        off = x - mean
        var = jnp.mean(off * off, axis=-1, keepdims=True)
        normed[r * length : (r + 1) * length] = (off / jnp.sqrt(var + 1e-05) * gain_ref[...]).astype(BF)
    pos = pos_ref[0]
    for c in range(3):
        y = jnp.dot(normed[...], w_ref[c], preferred_element_type=F32)
        for h in range(heads):
            mine[h] = jnp.concatenate(
                [y[r * length : (r + 1) * length, h * HEAD_DIM : (h + 1) * HEAD_DIM] for r in range(seqs)], axis=1
            ).astype(BF)
        for s in range(RING):
            outs[c * RING + s][...] = mine[head_at(pos + s)]


def gather_kernel(pos_ref, *refs):
    parts, out = refs[:-1], refs[-1]
    pos = pos_ref[0]
    for s in range(RING):
        src = lax.rem(pos + RING - s, RING)
        out[lax.div(src, Z), lax.rem(src, Z)] = parts[s][...]


def logits_kernel(pos_ref, *refs):
    q_parts, (k_ref, k_far, out_ref, q) = refs[:RING], refs[RING:]
    pos = pos_ref[0]
    for s in range(RING):
        src = lax.rem(pos + RING - s, RING)
        q[lax.div(src, Z), lax.rem(src, Z)] = q_parts[s][...]
    half = k_ref.shape[1] * k_ref.shape[2]
    for side, keys in enumerate((k_ref, k_far)):
        total = None
        for w in range(W):
            a = q[w].reshape(half, -1)
            b = keys[w].reshape(half, -1)
            term = lax.dot_general(a, b, (((1,), (1,)), ((), ())), preferred_element_type=F32)
            total = term if total is None else total + term
        out_ref[:, side * half : (side + 1) * half] = total.astype(BF)


def probs_kernel(scale, x_ref, out_ref):
    logits = x_ref[0].astype(F32)
    for i in range(1, x_ref.shape[0]):
        logits = logits + x_ref[i].astype(F32)
    expo = jnp.exp(logits * scale)
    probs = (expo / jnp.sum(expo, axis=-1, keepdims=True)).astype(BF)
    for i in range(out_ref.shape[0]):
        out_ref[i] = probs


def context_kernel(pos_ref, p_ref, v_ref, v_far, *refs):
    outs, mine = refs[:-1], refs[-1]
    half = v_ref.shape[1] * v_ref.shape[2]
    length = v_ref.shape[2]
    for w in range(W):
        a = jnp.dot(p_ref[:, :half], v_ref[w].reshape(half, -1), preferred_element_type=F32)
        a = a + jnp.dot(p_ref[:, half:], v_far[w].reshape(half, -1), preferred_element_type=F32)
        a = a.astype(BF)
        for z in range(Z):
            mine[w * Z + z] = a[z * length : (z + 1) * length]
    pos = pos_ref[0]
    for s in range(RING):
        outs[s][...] = mine[lax.rem(pos + s, RING)]


def mix_kernel(pos_ref, w_ref, *refs):
    parts, (out_ref, rows) = refs[:-2], refs[-2:]
    pos = pos_ref[0]
    for s in range(RING):
        h = head_at(pos + RING - s)
        rows[s * HEAD_DIM : (s + 1) * HEAD_DIM] = w_ref[pl.ds(pl.multiple_of(h * HEAD_DIM, HEAD_DIM), HEAD_DIM)]
    for r in range(out_ref.shape[0]):
        lhs = jnp.concatenate([part[:, r * HEAD_DIM : (r + 1) * HEAD_DIM] for part in parts], axis=1)
        out_ref[r] = jnp.dot(lhs, rows[...], preferred_element_type=F32)


def call(kernel, out_shape, operands, scratch=(), flops=0):
    moved = sum(math.prod(o.shape) * o.dtype.itemsize for o in operands)
    return pl.pallas_call(
        kernel,
        out_shape=out_shape,
        in_specs=[SMEM if o.dtype == jnp.int32 else VMEM for o in operands],
        out_specs=jax.tree.map(lambda _: VMEM, out_shape),
        scratch_shapes=list(scratch),
        compiler_params=PARAMS,
        cost_estimate=pl.CostEstimate(flops=flops, bytes_accessed=2 * moved, transcendentals=0),
    )(*operands)


def along_ring(parts):
    got = [parts[0]] + [None] * (RING - 1)
    for s in (4, 3, 5, 2, 6, 1, 7):
        pairs = [(i, index_of((place(i) + s) % RING)) for i in range(RING)]
        got[s] = lax.ppermute(parts[s], ("z", "w"), pairs)
    return got


def other_core(a):
    return lax.ppermute(a, "c", [(0, 1), (1, 0)])


def shards(tokens, ln_gain, w_qkv, w_out):
    seqs, length, width = tokens.shape
    inner = w_qkv.shape[2]
    lanes = seqs * HEAD_DIM
    pos = (lax.axis_index("w") * Z + lax.axis_index("z")).astype(jnp.int32).reshape(1)
    block = jax.ShapeDtypeStruct((length, lanes), BF)
    whole = jax.ShapeDtypeStruct((W, Z, length, lanes), BF)
    half = Z * length
    full = CORE * half
    scale = 1.0 / math.sqrt(HEAD_DIM * seqs * W * PLANE)

    outs = call(
        project_kernel,
        [block] * (3 * RING),
        [pos, tokens, ln_gain.reshape(1, width), jnp.transpose(w_qkv, (1, 0, 2))],
        [pltpu.VMEM((seqs * length, width), BF), pltpu.VMEM((RING, length, lanes), BF)],
        flops=2 * seqs * length * width * 3 * inner,
    )
    query, keys, values = outs[:RING], outs[RING : 2 * RING], outs[2 * RING :]
    keys = along_ring(keys)
    query = along_ring(query)
    values = along_ring(values)
    keys = call(gather_kernel, whole, [pos, *keys])
    keys_far = other_core(keys)
    term = call(
        logits_kernel,
        jax.ShapeDtypeStruct((half, full), BF),
        [pos, *query, keys, keys_far],
        [pltpu.VMEM(whole.shape, BF)],
        flops=2 * half * full * W * lanes,
    )
    chunk = (PLANE, half // PLANE, full)
    terms = lax.all_to_all(term.reshape(chunk), ("x", "y"), 0, 0, tiled=True)
    probs = call(functools.partial(probs_kernel, scale), jax.ShapeDtypeStruct(chunk, BF), [terms])
    probs = lax.all_to_all(probs, ("x", "y"), 0, 0, tiled=True).reshape(half, full)
    values = call(gather_kernel, whole, [pos, *values])
    values_far = other_core(values)
    context = call(
        context_kernel,
        [block] * RING,
        [pos, probs, values, values_far],
        [pltpu.VMEM((RING, length, lanes), BF)],
        flops=2 * half * full * W * lanes,
    )
    context = along_ring(context)
    return call(
        mix_kernel,
        jax.ShapeDtypeStruct((seqs, length, width), F32),
        [pos, w_out, *context],
        [pltpu.VMEM(w_out.shape, BF)],
        flops=2 * seqs * length * inner * width,
    )


def solution(mesh):
    cut = Mesh(mesh.devices.reshape(Z, CORE, X, Y, W), ("z", "c", "x", "y", "w"))
    split = P(("x", "y", "w"), ("z", "c"), None)
    return jax.shard_map(shards, mesh=cut, in_specs=(split, P(), P(), P()), out_specs=split, check_vma=False)
```

```python
import functools
import math

import jax
import jax.numpy as jnp
from jax import lax
from jax.experimental import pallas as pl
from jax.experimental.pallas import tpu as pltpu
from jax.sharding import Mesh
from jax.sharding import PartitionSpec as P

HEAD_DIM = 64
Z, CORE, X, Y, W = 4, 2, 4, 4, 2
RING = Z * W
PLANE = X * Y
BF = jnp.bfloat16
F32 = jnp.float32
VMEM = pl.BlockSpec(memory_space=pltpu.VMEM)
SMEM = pl.BlockSpec(memory_space=pltpu.SMEM)
PARAMS = pltpu.CompilerParams(vmem_limit_bytes=48 * 1024 * 1024)


def place(index):
    return (index % W) * Z + index // W


def index_of(position):
    return (position % Z) * W + position // Z


def head_at(position):
    pos = lax.rem(position, RING)
    return lax.rem(pos, Z) * W + lax.div(pos, Z)


def project_kernel(pos_ref, x_ref, gain_ref, w_ref, *refs):
    both, values, (normed, mine) = refs[:RING], refs[RING:-2], refs[-2:]
    seqs, length, width = x_ref.shape
    inner = w_ref.shape[2]
    heads = inner // HEAD_DIM
    gain = gain_ref[...].reshape(1, width)
    for r in range(seqs):
        x = x_ref[r].astype(F32)
        mean = jnp.mean(x, axis=-1, keepdims=True)
        off = x - mean
        var = jnp.mean(off * off, axis=-1, keepdims=True)
        normed[r * length : (r + 1) * length] = (off / jnp.sqrt(var + 1e-05) * gain).astype(BF)
    pos = pos_ref[0]
    for c in (1, 0, 2):
        y = jnp.dot(normed[...], w_ref[c], preferred_element_type=F32)
        for h in range(heads):
            mine[h] = jnp.concatenate(
                [y[r * length : (r + 1) * length, h * HEAD_DIM : (h + 1) * HEAD_DIM] for r in range(seqs)], axis=1
            ).astype(BF)
        for s in range(RING):
            block = mine[head_at(pos + s)]
            if c == 2:
                values[s][...] = block
            else:
                both[s][(1 - c) * length : (2 - c) * length] = block


def put_by_sender(pos, parts, first, out):
    length = out.shape[2]
    for s in range(RING):
        src = lax.rem(pos + RING - s, RING)
        out[lax.div(src, Z), lax.rem(src, Z)] = parts[s][first : first + length]


def keys_kernel(pos_ref, *refs):
    put_by_sender(pos_ref[0], refs[:-1], 0, refs[-1])


def logits_kernel(pos_ref, *refs):
    parts, (k_ref, k_far, out_ref, q) = refs[:RING], refs[RING:]
    put_by_sender(pos_ref[0], parts, q.shape[2], q)
    half = k_ref.shape[1] * k_ref.shape[2]
    for side, keys in enumerate((k_ref, k_far)):
        total = None
        for w in range(W):
            a = q[w].reshape(half, -1)
            b = keys[w].reshape(half, -1)
            term = lax.dot_general(a, b, (((1,), (1,)), ((), ())), preferred_element_type=F32)
            total = term if total is None else total + term
        out_ref[:, side * half : (side + 1) * half] = total.astype(BF)


def probs_kernel(scale, pos_ref, x_ref, *refs):
    parts, (out_ref, values) = refs[:RING], refs[RING:]
    put_by_sender(pos_ref[0], parts, 0, values)
    logits = x_ref[0].astype(F32)
    for i in range(1, x_ref.shape[0]):
        logits = logits + x_ref[i].astype(F32)
    expo = jnp.exp(logits * scale)
    probs = (expo / jnp.sum(expo, axis=-1, keepdims=True)).astype(BF)
    for i in range(out_ref.shape[0]):
        out_ref[i] = probs


def context_kernel(pos_ref, p_ref, v_ref, v_far, *refs):
    outs, mine = refs[:-1], refs[-1]
    half = v_ref.shape[1] * v_ref.shape[2]
    length = v_ref.shape[2]
    for w in range(W):
        a = jnp.dot(p_ref[:, :half], v_ref[w].reshape(half, -1), preferred_element_type=F32)
        a = a + jnp.dot(p_ref[:, half:], v_far[w].reshape(half, -1), preferred_element_type=F32)
        a = a.astype(BF)
        for z in range(Z):
            mine[w * Z + z] = a[z * length : (z + 1) * length]
    pos = pos_ref[0]
    for s in range(RING):
        outs[s][...] = mine[lax.rem(pos + s, RING)]


def mix_kernel(pos_ref, w_ref, *refs):
    parts, (out_ref, rows) = refs[:-2], refs[-2:]
    pos = pos_ref[0]
    for s in range(RING):
        h = head_at(pos + RING - s)
        rows[s * HEAD_DIM : (s + 1) * HEAD_DIM] = w_ref[pl.ds(pl.multiple_of(h * HEAD_DIM, HEAD_DIM), HEAD_DIM)]
    for r in range(out_ref.shape[0]):
        lhs = jnp.concatenate([part[:, r * HEAD_DIM : (r + 1) * HEAD_DIM] for part in parts], axis=1)
        out_ref[r] = jnp.dot(lhs, rows[...], preferred_element_type=F32)


def call(kernel, out_shape, operands, scratch=(), flops=0):
    moved = sum(math.prod(o.shape) * o.dtype.itemsize for o in operands)
    return pl.pallas_call(
        kernel,
        out_shape=out_shape,
        in_specs=[SMEM if o.dtype == jnp.int32 else VMEM for o in operands],
        out_specs=jax.tree.map(lambda _: VMEM, out_shape),
        scratch_shapes=list(scratch),
        compiler_params=PARAMS,
        cost_estimate=pl.CostEstimate(flops=flops, bytes_accessed=2 * moved, transcendentals=0),
    )(*operands)


def along_ring(parts):
    got = [parts[0]] + [None] * (RING - 1)
    for s in (4, 3, 5, 2, 6, 1, 7):
        pairs = [(i, index_of((place(i) + s) % RING)) for i in range(RING)]
        got[s] = lax.ppermute(parts[s], ("z", "w"), pairs)
    return got


def other_core(a):
    return lax.ppermute(a, "c", [(0, 1), (1, 0)])


def shards(tokens, ln_gain, w_qkv, w_out):
    seqs, length, width = tokens.shape
    inner = w_qkv.shape[2]
    lanes = seqs * HEAD_DIM
    pos = (lax.axis_index("w") * Z + lax.axis_index("z")).astype(jnp.int32).reshape(1)
    pair = jax.ShapeDtypeStruct((2 * length, lanes), BF)
    block = jax.ShapeDtypeStruct((length, lanes), BF)
    whole = jax.ShapeDtypeStruct((W, Z, length, lanes), BF)
    half = Z * length
    full = CORE * half
    scale = 1.0 / math.sqrt(HEAD_DIM * seqs * W * PLANE)

    outs = call(
        project_kernel,
        [pair] * RING + [block] * RING,
        [pos, tokens, ln_gain, jnp.transpose(w_qkv, (1, 0, 2))],
        [pltpu.VMEM((seqs * length, width), BF), pltpu.VMEM((RING, length, lanes), BF)],
        flops=2 * seqs * length * width * 3 * inner,
    )
    both = along_ring(outs[:RING])
    values = along_ring(outs[RING:])
    keys = call(keys_kernel, whole, [pos, *both])
    keys_far = other_core(keys)
    term = call(
        logits_kernel,
        jax.ShapeDtypeStruct((half, full), BF),
        [pos, *both, keys, keys_far],
        [pltpu.VMEM(whole.shape, BF)],
        flops=2 * half * full * W * lanes,
    )
    chunk = (PLANE, half // PLANE, full)
    terms = lax.all_to_all(term.reshape(chunk), ("x", "y"), 0, 0, tiled=True)
    probs, values = call(
        functools.partial(probs_kernel, scale),
        [jax.ShapeDtypeStruct(chunk, BF), whole],
        [pos, terms, *values],
    )
    probs = lax.all_to_all(probs, ("x", "y"), 0, 0, tiled=True).reshape(half, full)
    values_far = other_core(values)
    context = call(
        context_kernel,
        [block] * RING,
        [pos, probs, values, values_far],
        [pltpu.VMEM((RING, length, lanes), BF)],
        flops=2 * half * full * W * lanes,
    )
    context = along_ring(context)
    return call(
        mix_kernel,
        jax.ShapeDtypeStruct((seqs, length, width), F32),
        [pos, w_out, *context],
        [pltpu.VMEM(w_out.shape, BF)],
        flops=2 * seqs * length * inner * width,
    )


def solution(mesh):
    cut = Mesh(mesh.devices.reshape(Z, CORE, X, Y, W), ("z", "c", "x", "y", "w"))
    split = P(("x", "y", "w"), ("z", "c"), None)
    return jax.shard_map(shards, mesh=cut, in_specs=(split, P(), P(), P()), out_specs=split, check_vma=False)
```

```python
import functools
import math

import jax
import jax.numpy as jnp
from jax import lax
from jax.experimental import pallas as pl
from jax.experimental.pallas import tpu as pltpu
from jax.sharding import Mesh
from jax.sharding import PartitionSpec as P

HEAD_DIM = 64
Z, CORE, X, Y, W = 4, 2, 4, 4, 2
RING = Z * W
PLANE = X * Y
STEPS = (0, 4, 3, 5, 2, 6, 1, 7)
BF = jnp.bfloat16
F32 = jnp.float32
VMEM = pl.BlockSpec(memory_space=pltpu.VMEM)
HBM = pl.BlockSpec(memory_space=pltpu.HBM)
ANY = pl.BlockSpec(memory_space=pl.ANY)
SMEM = pl.BlockSpec(memory_space=pltpu.SMEM)
MIB = 1024 * 1024


def place(index):
    return (index % W) * Z + index // W


def index_of(position):
    return (position % Z) * W + position // Z


def head_at(position):
    pos = lax.rem(position, RING)
    return lax.rem(pos, Z) * W + lax.div(pos, Z)


def blocks_by_head(y, seqs, mine):
    length = y.shape[0] // seqs
    for h in range(mine.shape[0]):
        mine[h] = jnp.concatenate(
            [y[r * length : (r + 1) * length, h * HEAD_DIM : (h + 1) * HEAD_DIM] for r in range(seqs)], axis=1
        ).astype(BF)


def keys_queries_kernel(pos_ref, gain_ref, x_hbm, w_hbm, *refs):
    both, (normed, mine, x_ref, w_ref, x_sem, w_sem) = refs[:RING], refs[RING:]
    seqs, length, width = x_hbm.shape
    x_copies = [pltpu.make_async_copy(x_hbm.at[r], x_ref.at[r], x_sem.at[r]) for r in range(seqs)]
    w_copies = [pltpu.make_async_copy(w_hbm.at[c], w_ref.at[c], w_sem.at[c]) for c in range(2)]
    for copy in (*x_copies, w_copies[1], w_copies[0]):
        copy.start()
    gain = gain_ref[...].reshape(1, width)
    for r in range(seqs):
        x_copies[r].wait()
        x = x_ref[r].astype(F32)
        mean = jnp.mean(x, axis=-1, keepdims=True)
        off = x - mean
        var = jnp.mean(off * off, axis=-1, keepdims=True)
        normed[r * length : (r + 1) * length] = (off / jnp.sqrt(var + 1e-05) * gain).astype(BF)
    pos = pos_ref[0]
    for c in (1, 0):
        w_copies[c].wait()
        blocks_by_head(jnp.dot(normed[...], w_ref[c], preferred_element_type=F32), seqs, mine)
        for i, s in enumerate(STEPS):
            both[i][(1 - c) * length : (2 - c) * length] = mine[head_at(pos + s)]


def values_kernel(seqs, pos_ref, normed, w_hbm, *refs):
    outs, (mine, w_ref, w_sem) = refs[:RING], refs[RING:]
    copy = pltpu.make_async_copy(w_hbm.at[2], w_ref, w_sem)
    copy.start()
    copy.wait()
    blocks_by_head(jnp.dot(normed[...], w_ref[...], preferred_element_type=F32), seqs, mine)
    pos = pos_ref[0]
    for i, s in enumerate(STEPS):
        outs[i][...] = mine[head_at(pos + s)]


def put_by_sender(pos, parts, first, out):
    length = out.shape[2]
    for part, s in zip(parts, STEPS):
        src = lax.rem(pos + RING - s, RING)
        out[lax.div(src, Z), lax.rem(src, Z)] = part[first : first + length]


def place_kernel(pos_ref, *refs):
    put_by_sender(pos_ref[0], refs[:-1], 0, refs[-1])


def logits_kernel(pos_ref, *refs):
    parts, (k_ref, k_far, out_ref, q) = refs[:RING], refs[RING:]
    put_by_sender(pos_ref[0], parts, q.shape[2], q)
    half = k_ref.shape[1] * k_ref.shape[2]
    for side, keys in enumerate((k_ref, k_far)):
        total = None
        for w in range(W):
            a = q[w].reshape(half, -1)
            b = keys[w].reshape(half, -1)
            term = lax.dot_general(a, b, (((1,), (1,)), ((), ())), preferred_element_type=F32)
            total = term if total is None else total + term
        out_ref[:, side * half : (side + 1) * half] = total.astype(BF)


def probs_kernel(scale, x_ref, *refs):
    out_ref = refs[-1]
    logits = x_ref[0].astype(F32)
    for i in range(1, x_ref.shape[0]):
        logits = logits + x_ref[i].astype(F32)
    expo = jnp.exp(logits * scale)
    probs = (expo / jnp.sum(expo, axis=-1, keepdims=True)).astype(BF)
    for i in range(out_ref.shape[0]):
        out_ref[i] = probs


def context_kernel(pos_ref, p_ref, v_ref, far_hbm, *refs):
    outs, (mine, v_far, sem) = refs[:RING], refs[RING:]
    copy = pltpu.make_async_copy(far_hbm, v_far, sem)
    copy.start()
    half = v_ref.shape[1] * v_ref.shape[2]
    length = v_ref.shape[2]
    near = [jnp.dot(p_ref[:, :half], v_ref[w].reshape(half, -1), preferred_element_type=F32) for w in range(W)]
    copy.wait()
    for w in range(W):
        a = near[w] + jnp.dot(p_ref[:, half:], v_far[w].reshape(half, -1), preferred_element_type=F32)
        a = a.astype(BF)
        for z in range(Z):
            mine[w * Z + z] = a[z * length : (z + 1) * length]
    pos = pos_ref[0]
    for i, s in enumerate(STEPS):
        outs[i][...] = mine[lax.rem(pos + s, RING)]


def mix_kernel(pos_ref, w_ref, *refs):
    parts, (out_hbm, rows, mixed, sem) = refs[:RING], refs[RING:]
    pos = pos_ref[0]
    for i, s in enumerate(STEPS):
        h = head_at(pos + RING - s)
        rows[i * HEAD_DIM : (i + 1) * HEAD_DIM] = w_ref[pl.ds(pl.multiple_of(h * HEAD_DIM, HEAD_DIM), HEAD_DIM)]
    copies = []
    for r in range(mixed.shape[0]):
        lhs = jnp.concatenate([part[:, r * HEAD_DIM : (r + 1) * HEAD_DIM] for part in parts], axis=1)
        mixed[r] = jnp.dot(lhs, rows[...], preferred_element_type=F32)
        copies.append(pltpu.make_async_copy(mixed.at[r], out_hbm.at[r], sem.at[r]))
        copies[r].start()
    for copy in copies:
        copy.wait()


def call(kernel, out_shape, operands, scratch=(), flops=0, hbm=(), unread=(), out_specs=None, vmem=20):
    moved = sum(math.prod(o.shape) * o.dtype.itemsize for o in operands)
    specs = [
        SMEM if o.dtype == jnp.int32 else HBM if i in hbm else ANY if i in unread else VMEM for i, o in enumerate(operands)
    ]
    return pl.pallas_call(
        kernel,
        out_shape=out_shape,
        in_specs=specs,
        out_specs=out_specs or jax.tree.map(lambda _: VMEM, out_shape),
        scratch_shapes=list(scratch),
        compiler_params=pltpu.CompilerParams(vmem_limit_bytes=vmem * MIB),
        cost_estimate=pl.CostEstimate(flops=flops, bytes_accessed=2 * moved, transcendentals=0),
    )(*operands)


def along_ring(parts):
    got = []
    for part, s in zip(parts, STEPS):
        pairs = [(i, index_of((place(i) + s) % RING)) for i in range(RING)]
        got.append(lax.ppermute(part, ("z", "w"), pairs) if s else part)
    return got


def other_core(a):
    return lax.ppermute(a, "c", [(0, 1), (1, 0)])


def shards(tokens, ln_gain, w_qkv, w_out):
    seqs, length, width = tokens.shape
    inner = w_qkv.shape[2]
    lanes = seqs * HEAD_DIM
    pos = (lax.axis_index("w") * Z + lax.axis_index("z")).astype(jnp.int32).reshape(1)
    pair = jax.ShapeDtypeStruct((2 * length, lanes), BF)
    block = jax.ShapeDtypeStruct((length, lanes), BF)
    whole = jax.ShapeDtypeStruct((W, Z, length, lanes), BF)
    half = Z * length
    full = CORE * half
    scale = 1.0 / math.sqrt(HEAD_DIM * seqs * W * PLANE)

    weights = jnp.transpose(w_qkv, (1, 0, 2))
    dma = pltpu.SemaphoreType.DMA
    *both, normed = call(
        keys_queries_kernel,
        [pair] * RING + [jax.ShapeDtypeStruct((seqs * length, width), BF)],
        [pos, ln_gain, tokens, weights],
        [
            pltpu.VMEM((RING, length, lanes), BF),
            pltpu.VMEM(tokens.shape, BF),
            pltpu.VMEM((2, width, inner), BF),
            dma((seqs,)),
            dma((2,)),
        ],
        flops=2 * seqs * length * width * 2 * inner,
        hbm=(2, 3),
        vmem=57,
    )
    both = along_ring(both)
    values = call(
        functools.partial(values_kernel, seqs),
        [block] * RING,
        [pos, normed, weights],
        [pltpu.VMEM((RING, length, lanes), BF), pltpu.VMEM((width, inner), BF), dma],
        flops=2 * seqs * length * width * inner,
        hbm=(2,),
        vmem=20,
    )
    values = along_ring(values)
    keys = call(place_kernel, whole, [pos, *both])
    keys_far = other_core(keys)
    term = call(
        logits_kernel,
        jax.ShapeDtypeStruct((half, full), BF),
        [pos, *both, keys, keys_far],
        [pltpu.VMEM(whole.shape, BF)],
        flops=2 * half * full * W * lanes,
    )
    chunk = (PLANE, half // PLANE, full)
    terms = lax.all_to_all(term.reshape(chunk), ("x", "y"), 0, 0, tiled=True)
    early = values[1:5]
    probs = call(
        functools.partial(probs_kernel, scale),
        jax.ShapeDtypeStruct(chunk, BF),
        [terms, *early],
        unread=range(1, 5),
    )
    probs = lax.all_to_all(probs, ("x", "y"), 0, 0, tiled=True).reshape(half, full)
    values = call(place_kernel, whole, [pos, *values])
    values_far = other_core(values)
    context = call(
        context_kernel,
        [block] * RING,
        [pos, probs, values, values_far],
        [pltpu.VMEM((RING, length, lanes), BF), pltpu.VMEM(whole.shape, BF), dma],
        flops=2 * half * full * W * lanes,
        hbm=(3,),
        vmem=20,
    )
    context = along_ring(context)
    return call(
        mix_kernel,
        jax.ShapeDtypeStruct((seqs, length, width), F32),
        [pos, w_out, *context],
        [pltpu.VMEM(w_out.shape, BF), pltpu.VMEM((seqs, length, width), F32), dma((seqs,))],
        flops=2 * seqs * length * inner * width,
        out_specs=HBM,
    )


def solution(mesh):
    cut = Mesh(mesh.devices.reshape(Z, CORE, X, Y, W), ("z", "c", "x", "y", "w"))
    split = P(("x", "y", "w"), ("z", "c"), None)
    return jax.shard_map(shards, mesh=cut, in_specs=(split, P(), P(), P()), out_specs=split, check_vma=False)
```

```python
import functools
import math

import jax
import jax.numpy as jnp
from jax import lax
from jax.experimental import pallas as pl
from jax.experimental.pallas import tpu as pltpu
from jax.sharding import Mesh
from jax.sharding import PartitionSpec as P

HEAD_DIM = 64
Z, CORE, X, Y, W = 4, 2, 4, 4, 2
RING = Z * W
PLANE = X * Y
STEPS = (0, 4, 3, 5, 2, 6, 1, 7)
BF = jnp.bfloat16
F32 = jnp.float32
VMEM = pl.BlockSpec(memory_space=pltpu.VMEM)
HBM = pl.BlockSpec(memory_space=pltpu.HBM)
ANY = pl.BlockSpec(memory_space=pl.ANY)
SMEM = pl.BlockSpec(memory_space=pltpu.SMEM)
MIB = 1024 * 1024


def place(index):
    return (index % W) * Z + index // W


def index_of(position):
    return (position % Z) * W + position // Z


def head_at(position):
    pos = lax.rem(position, RING)
    return lax.rem(pos, Z) * W + lax.div(pos, Z)


def blocks_by_head(y, seqs, mine):
    length = y.shape[0] // seqs
    for h in range(mine.shape[0]):
        mine[h] = jnp.concatenate(
            [y[r * length : (r + 1) * length, h * HEAD_DIM : (h + 1) * HEAD_DIM] for r in range(seqs)], axis=1
        ).astype(BF)


def keys_queries_kernel(pos_ref, gain_hbm, x_hbm, w_hbm, *refs):
    both, (normed, mine, gain_ref, x_ref, w_ref, gain_sem, x_sem, w_sem) = refs[:RING], refs[RING:]
    seqs, length, width = x_hbm.shape
    x_copies = [pltpu.make_async_copy(x_hbm.at[r], x_ref.at[r], x_sem.at[r]) for r in range(seqs)]
    w_copies = [pltpu.make_async_copy(w_hbm.at[c], w_ref.at[c], w_sem.at[c]) for c in range(2)]
    gain_copy = pltpu.make_async_copy(gain_hbm, gain_ref, gain_sem)
    for copy in (x_copies[0], gain_copy, *x_copies[1:], w_copies[1], w_copies[0]):
        copy.start()
    gain_copy.wait()
    gain = gain_ref[...].reshape(1, width)
    for r in range(seqs):
        x_copies[r].wait()
        x = x_ref[r].astype(F32)
        mean = jnp.mean(x, axis=-1, keepdims=True)
        off = x - mean
        var = jnp.mean(off * off, axis=-1, keepdims=True)
        normed[r * length : (r + 1) * length] = (off / jnp.sqrt(var + 1e-05) * gain).astype(BF)
    pos = pos_ref[0]
    for c in (1, 0):
        w_copies[c].wait()
        blocks_by_head(jnp.dot(normed[...], w_ref[c], preferred_element_type=F32), seqs, mine)
        for i, s in enumerate(STEPS):
            both[i][(1 - c) * length : (2 - c) * length] = mine[head_at(pos + s)]


def values_kernel(seqs, pos_ref, normed, w_hbm, *refs):
    outs, (mine, w_ref, w_sem) = refs[:RING], refs[RING:]
    copy = pltpu.make_async_copy(w_hbm.at[2], w_ref, w_sem)
    copy.start()
    copy.wait()
    blocks_by_head(jnp.dot(normed[...], w_ref[...], preferred_element_type=F32), seqs, mine)
    pos = pos_ref[0]
    for i, s in enumerate(STEPS):
        outs[i][...] = mine[head_at(pos + s)]


def put_by_sender(pos, parts, first, out):
    length = out.shape[2]
    for part, s in zip(parts, STEPS):
        src = lax.rem(pos + RING - s, RING)
        out[lax.div(src, Z), lax.rem(src, Z)] = part[first : first + length]


def place_kernel(count, pos_ref, *refs):
    put_by_sender(pos_ref[0], refs[:count], 0, refs[-1])


def logits_kernel(pos_ref, *refs):
    parts, (k_ref, k_far, out_hbm, q, terms, sem) = refs[:RING], refs[RING:]
    put_by_sender(pos_ref[0], parts, q.shape[2], q)
    length = k_ref.shape[2]
    half = k_ref.shape[1] * length
    copies = []
    for z in range(Z):
        rows = slice(z * length, (z + 1) * length)
        for side, keys in enumerate((k_ref, k_far)):
            total = None
            for w in range(W):
                term = lax.dot_general(
                    q[w, z], keys[w].reshape(half, -1), (((1,), (1,)), ((), ())), preferred_element_type=F32
                )
                total = term if total is None else total + term
            terms[rows, side * half : (side + 1) * half] = total.astype(BF)
        copies.append(pltpu.make_async_copy(terms.at[rows], out_hbm.at[rows], sem.at[z]))
        copies[z].start()
    for copy in copies:
        copy.wait()


def probs_kernel(scale, x_ref, *refs):
    out_ref = refs[-1]
    logits = x_ref[0].astype(F32)
    for i in range(1, x_ref.shape[0]):
        logits = logits + x_ref[i].astype(F32)
    expo = jnp.exp(logits * scale)
    probs = (expo / jnp.sum(expo, axis=-1, keepdims=True)).astype(BF)
    for i in range(out_ref.shape[0]):
        out_ref[i] = probs


def context_kernel(pos_ref, p_ref, v_ref, far_hbm, *refs):
    outs, (mine, v_far, sem) = refs[:RING], refs[RING:]
    copy = pltpu.make_async_copy(far_hbm, v_far, sem)
    copy.start()
    half = v_ref.shape[1] * v_ref.shape[2]
    length = v_ref.shape[2]
    near = [jnp.dot(p_ref[:, :half], v_ref[w].reshape(half, -1), preferred_element_type=F32) for w in range(W)]
    copy.wait()
    for w in range(W):
        a = near[w] + jnp.dot(p_ref[:, half:], v_far[w].reshape(half, -1), preferred_element_type=F32)
        a = a.astype(BF)
        for z in range(Z):
            mine[w * Z + z] = a[z * length : (z + 1) * length]
    pos = pos_ref[0]
    for i, s in enumerate(STEPS):
        outs[i][...] = mine[lax.rem(pos + s, RING)]


def mix_kernel(pos_ref, w_ref, *refs):
    parts, (out_hbm, rows, mixed, sem) = refs[:RING], refs[RING:]
    pos = pos_ref[0]
    for i, s in enumerate(STEPS):
        h = head_at(pos + RING - s)
        rows[i * HEAD_DIM : (i + 1) * HEAD_DIM] = w_ref[pl.ds(pl.multiple_of(h * HEAD_DIM, HEAD_DIM), HEAD_DIM)]
    copies = []
    for r in range(mixed.shape[0]):
        lhs = jnp.concatenate([part[:, r * HEAD_DIM : (r + 1) * HEAD_DIM] for part in parts], axis=1)
        mixed[r] = jnp.dot(lhs, rows[...], preferred_element_type=F32)
        copies.append(pltpu.make_async_copy(mixed.at[r], out_hbm.at[r], sem.at[r]))
        copies[r].start()
    for copy in copies:
        copy.wait()


def call(kernel, out_shape, operands, scratch=(), flops=0, hbm=(), unread=(), out_specs=None, vmem=20):
    moved = sum(math.prod(o.shape) * o.dtype.itemsize for o in operands)
    specs = [
        SMEM if o.dtype == jnp.int32 else HBM if i in hbm else ANY if i in unread else VMEM for i, o in enumerate(operands)
    ]
    return pl.pallas_call(
        kernel,
        out_shape=out_shape,
        in_specs=specs,
        out_specs=out_specs or jax.tree.map(lambda _: VMEM, out_shape),
        scratch_shapes=list(scratch),
        compiler_params=pltpu.CompilerParams(vmem_limit_bytes=vmem * MIB),
        cost_estimate=pl.CostEstimate(flops=flops, bytes_accessed=2 * moved, transcendentals=0),
    )(*operands)


def along_ring(parts):
    got = []
    for part, s in zip(parts, STEPS):
        pairs = [(i, index_of((place(i) + s) % RING)) for i in range(RING)]
        got.append(lax.ppermute(part, ("z", "w"), pairs) if s else part)
    return got


def other_core(a):
    return lax.ppermute(a, "c", [(0, 1), (1, 0)])


def shards(tokens, ln_gain, w_qkv, w_out):
    seqs, length, width = tokens.shape
    inner = w_qkv.shape[2]
    lanes = seqs * HEAD_DIM
    pos = (lax.axis_index("w") * Z + lax.axis_index("z")).astype(jnp.int32).reshape(1)
    pair = jax.ShapeDtypeStruct((2 * length, lanes), BF)
    block = jax.ShapeDtypeStruct((length, lanes), BF)
    whole = jax.ShapeDtypeStruct((W, Z, length, lanes), BF)
    half = Z * length
    full = CORE * half
    scale = 1.0 / math.sqrt(HEAD_DIM * seqs * W * PLANE)

    weights = jnp.transpose(w_qkv, (1, 0, 2))
    dma = pltpu.SemaphoreType.DMA
    *both, normed = call(
        keys_queries_kernel,
        [pair] * RING + [jax.ShapeDtypeStruct((seqs * length, width), BF)],
        [pos, ln_gain, tokens, weights],
        [
            pltpu.VMEM((RING, length, lanes), BF),
            pltpu.VMEM(ln_gain.shape, F32),
            pltpu.VMEM(tokens.shape, BF),
            pltpu.VMEM((2, width, inner), BF),
            dma,
            dma((seqs,)),
            dma((2,)),
        ],
        flops=2 * seqs * length * width * 2 * inner,
        hbm=(1, 2, 3),
        vmem=51,
    )
    both = along_ring(both)
    values = call(
        functools.partial(values_kernel, seqs),
        [block] * RING,
        [pos, normed, weights],
        [pltpu.VMEM((RING, length, lanes), BF), pltpu.VMEM((width, inner), BF), dma],
        flops=2 * seqs * length * width * inner,
        hbm=(2,),
        vmem=20,
    )
    keys = call(functools.partial(place_kernel, RING), whole, [pos, *both, values[0]], unread=(1 + RING,))
    keys_far = other_core(keys)
    values = along_ring(values)
    term = call(
        logits_kernel,
        jax.ShapeDtypeStruct((half, full), BF),
        [pos, *both, keys, keys_far],
        [pltpu.VMEM(whole.shape, BF), pltpu.VMEM((half, full), BF), dma((Z,))],
        flops=2 * half * full * W * lanes,
        out_specs=HBM,
    )
    chunk = (PLANE, half // PLANE, full)
    terms = lax.all_to_all(term.reshape(chunk), ("x", "y"), 0, 0, tiled=True)
    early = values[1:5]
    probs = call(
        functools.partial(probs_kernel, scale),
        jax.ShapeDtypeStruct(chunk, BF),
        [terms, *early],
        unread=range(1, 5),
    )
    probs = lax.all_to_all(probs, ("x", "y"), 0, 0, tiled=True).reshape(half, full)
    values = call(functools.partial(place_kernel, RING), whole, [pos, *values])
    values_far = other_core(values)
    context = call(
        context_kernel,
        [block] * RING,
        [pos, probs, values, values_far],
        [pltpu.VMEM((RING, length, lanes), BF), pltpu.VMEM(whole.shape, BF), dma],
        flops=2 * half * full * W * lanes,
        hbm=(3,),
        vmem=20,
    )
    context = along_ring(context)
    return call(
        mix_kernel,
        jax.ShapeDtypeStruct((seqs, length, width), F32),
        [pos, w_out, *context],
        [pltpu.VMEM(w_out.shape, BF), pltpu.VMEM((seqs, length, width), F32), dma((seqs,))],
        flops=2 * seqs * length * inner * width,
        out_specs=HBM,
    )


def solution(mesh):
    cut = Mesh(mesh.devices.reshape(Z, CORE, X, Y, W), ("z", "c", "x", "y", "w"))
    split = P(("x", "y", "w"), ("z", "c"), None)
    return jax.shard_map(shards, mesh=cut, in_specs=(split, P(), P(), P()), out_specs=split, check_vma=False)
```

```python
import functools
import math

import jax
import jax.numpy as jnp
from jax import lax
from jax.experimental import pallas as pl
from jax.experimental.pallas import tpu as pltpu
from jax.sharding import Mesh
from jax.sharding import PartitionSpec as P

HEAD_DIM = 64
Z, CORE, X, Y, W = 4, 2, 4, 4, 2
RING = Z * W
PLANE = X * Y
STEPS = (0, 4, 3, 5, 2, 6, 1, 7)
BF = jnp.bfloat16
F32 = jnp.float32
VMEM = pl.BlockSpec(memory_space=pltpu.VMEM)
HBM = pl.BlockSpec(memory_space=pltpu.HBM)
ANY = pl.BlockSpec(memory_space=pl.ANY)
SMEM = pl.BlockSpec(memory_space=pltpu.SMEM)
X_STEPS = (0, 2, 1, 3)
Y_STEPS = (0, 1, 3, 2)
EARLY = 6
MIB = 1024 * 1024


def place(index):
    return (index % W) * Z + index // W


def index_of(position):
    return (position % Z) * W + position // Z


def head_at(position):
    pos = lax.rem(position, RING)
    return lax.rem(pos, Z) * W + lax.div(pos, Z)


def blocks_by_head(y, seqs, mine):
    length = y.shape[0] // seqs
    for h in range(mine.shape[0]):
        mine[h] = jnp.concatenate(
            [y[r * length : (r + 1) * length, h * HEAD_DIM : (h + 1) * HEAD_DIM] for r in range(seqs)], axis=1
        ).astype(BF)


def keys_queries_kernel(pos_ref, gain_hbm, x_hbm, w_hbm, *refs):
    both, (normed, mine, gain_ref, x_ref, w_ref, gain_sem, x_sem, w_sem) = refs[:RING], refs[RING:]
    seqs, length, width = x_hbm.shape
    x_copies = [pltpu.make_async_copy(x_hbm.at[r], x_ref.at[r], x_sem.at[r]) for r in range(seqs)]
    w_copies = [pltpu.make_async_copy(w_hbm.at[c], w_ref.at[c], w_sem.at[c]) for c in range(2)]
    gain_copy = pltpu.make_async_copy(gain_hbm, gain_ref, gain_sem)
    for copy in (x_copies[0], gain_copy, *x_copies[1:], w_copies[1], w_copies[0]):
        copy.start()
    gain_copy.wait()
    gain = gain_ref[...].reshape(1, width)
    for r in range(seqs):
        x_copies[r].wait()
        x = x_ref[r].astype(F32)
        mean = jnp.mean(x, axis=-1, keepdims=True)
        off = x - mean
        var = jnp.mean(off * off, axis=-1, keepdims=True)
        normed[r * length : (r + 1) * length] = (off / jnp.sqrt(var + 1e-05) * gain).astype(BF)
    pos = pos_ref[0]
    for c in (1, 0):
        w_copies[c].wait()
        blocks_by_head(jnp.dot(normed[...], w_ref[c], preferred_element_type=F32), seqs, mine)
        for i, s in enumerate(STEPS):
            both[i][(1 - c) * length : (2 - c) * length] = mine[head_at(pos + s)]


def values_kernel(seqs, pos_ref, normed, w_hbm, *refs):
    outs, (mine, w_ref, w_sem) = refs[:RING], refs[RING:]
    copy = pltpu.make_async_copy(w_hbm.at[2], w_ref, w_sem)
    copy.start()
    copy.wait()
    blocks_by_head(jnp.dot(normed[...], w_ref[...], preferred_element_type=F32), seqs, mine)
    pos = pos_ref[0]
    for i, s in enumerate(STEPS):
        outs[i][...] = mine[head_at(pos + s)]


def put_by_sender(pos, parts, first, out):
    length = out.shape[2]
    for part, s in zip(parts, STEPS):
        src = lax.rem(pos + RING - s, RING)
        out[lax.div(src, Z), -s % Z] = part[first : first + length]


def place_kernel(count, pos_ref, *refs):
    put_by_sender(pos_ref[0], refs[:count], 0, refs[-1])


def logits_kernel(pos_ref, *refs):
    parts, (k_ref, k_far, out_hbm, q, terms, sem) = refs[:RING], refs[RING:]
    put_by_sender(pos_ref[0], parts, q.shape[2], q)
    length = k_ref.shape[2]
    half = k_ref.shape[1] * length
    rows = terms.shape[1]
    copies = []
    for side, keys in enumerate((k_ref, k_far)):
        total = None
        for w in range(W):
            term = lax.dot_general(
                q[w].reshape(half, -1),
                keys[w].reshape(half, -1),
                (((1,), (1,)), ((), ())),
                preferred_element_type=F32,
            )
            total = term if total is None else total + term
        columns = slice(side * half, (side + 1) * half)
        for t in range(Z):
            for x in range(X):
                first = t * length + x * rows
                terms[x * Y + t, :, columns] = total[first : first + rows].astype(BF)
        copies.append(pltpu.make_async_copy(terms.at[:, :, columns], out_hbm.at[:, :, columns], sem.at[side]))
        copies[side].start()
    for copy in copies:
        copy.wait()


def probs_kernel(scale, x_ref, *refs):
    out_ref = refs[-1]
    logits = x_ref[0].astype(F32)
    for i in range(1, x_ref.shape[0]):
        logits = logits + x_ref[i].astype(F32)
    expo = jnp.exp(logits * scale)
    out_ref[...] = (expo / jnp.sum(expo, axis=-1, keepdims=True)).astype(BF)


def rows_kernel(pos_ref, *refs):
    parts, out = refs[:-1], refs[-1]
    for s, part in zip(X_STEPS, parts):
        out[lax.rem(pos_ref[1] + X - s, X)] = part[...]


def context_kernel(step, pos_ref, p_ref, v_ref, v_far, near, far, mine):
    half = v_ref.shape[1] * v_ref.shape[2]
    for w in range(W):
        a = jnp.dot(p_ref[:, :half], v_ref[w].reshape(half, -1), preferred_element_type=F32)
        a = a + jnp.dot(p_ref[:, half:], v_far[w].reshape(half, -1), preferred_element_type=F32)
        mine[w] = a.astype(BF)
    block = lax.rem(pos_ref[2] + Y - step, Y)
    run = lax.div(lax.rem(pos_ref[0] + block, RING), Z)
    near[...] = mine[run]
    far[...] = mine[1 - run]


def mix_kernel(pos_ref, w_ref, *refs):
    parts, (out_hbm, rows, mixed, sem) = refs[:RING], refs[RING:]
    for i in range(RING):
        block = lax.rem(pos_ref[2] + Y - Y_STEPS[i // W], Y)
        h = head_at(pos_ref[0] + RING - block - Z * (i % W))
        rows[i * HEAD_DIM : (i + 1) * HEAD_DIM] = w_ref[pl.ds(pl.multiple_of(h * HEAD_DIM, HEAD_DIM), HEAD_DIM)]
    copies = []
    for r in range(mixed.shape[0]):
        lhs = jnp.concatenate([part[:, r * HEAD_DIM : (r + 1) * HEAD_DIM] for part in parts], axis=1)
        mixed[r] = jnp.dot(lhs, rows[...], preferred_element_type=F32)
        copies.append(pltpu.make_async_copy(mixed.at[r], out_hbm.at[r], sem.at[r]))
        copies[r].start()
    for copy in copies:
        copy.wait()


def call(kernel, out_shape, operands, scratch=(), flops=0, hbm=(), unread=(), out_specs=None, vmem=20):
    moved = sum(math.prod(o.shape) * o.dtype.itemsize for o in operands)
    specs = [
        SMEM if o.dtype == jnp.int32 else HBM if i in hbm else ANY if i in unread else VMEM for i, o in enumerate(operands)
    ]
    return pl.pallas_call(
        kernel,
        out_shape=out_shape,
        in_specs=specs,
        out_specs=out_specs or jax.tree.map(lambda _: VMEM, out_shape),
        scratch_shapes=list(scratch),
        compiler_params=pltpu.CompilerParams(vmem_limit_bytes=vmem * MIB),
        cost_estimate=pl.CostEstimate(flops=flops, bytes_accessed=2 * moved, transcendentals=0),
    )(*operands)


def along_ring(parts):
    got = []
    for part, s in zip(parts, STEPS):
        pairs = [(i, index_of((place(i) + s) % RING)) for i in range(RING)]
        got.append(lax.ppermute(part, ("z", "w"), pairs) if s else part)
    return got


def along(a, axis, size, s):
    return lax.ppermute(a, axis, [(i, (i + s) % size) for i in range(size)]) if s else a


def to_block(part, step, more):
    pairs = []
    for i in range(Z * Y * W):
        z, y, w = i // (Y * W), i // W % Y, i % W
        there = index_of((place(z * W + w) + (y - step) % Y + more) % RING)
        pairs.append((i, (there // W * Y + y) * W + there % W))
    return lax.ppermute(part, ("z", "y", "w"), pairs)


def other_core(a):
    return lax.ppermute(a, "c", [(0, 1), (1, 0)])


def shards(tokens, ln_gain, w_qkv, w_out):
    seqs, length, width = tokens.shape
    inner = w_qkv.shape[2]
    lanes = seqs * HEAD_DIM
    ring = lax.axis_index("w") * Z + lax.axis_index("z")
    pos = jnp.stack([ring, lax.axis_index("x"), lax.axis_index("y")]).astype(jnp.int32)
    pair = jax.ShapeDtypeStruct((2 * length, lanes), BF)
    block = jax.ShapeDtypeStruct((length, lanes), BF)
    whole = jax.ShapeDtypeStruct((W, Z, length, lanes), BF)
    half = Z * length
    full = CORE * half
    scale = 1.0 / math.sqrt(HEAD_DIM * seqs * W * PLANE)

    weights = jnp.transpose(w_qkv, (1, 0, 2))
    dma = pltpu.SemaphoreType.DMA
    *both, normed = call(
        keys_queries_kernel,
        [pair] * RING + [jax.ShapeDtypeStruct((seqs * length, width), BF)],
        [pos, ln_gain, tokens, weights],
        [
            pltpu.VMEM((RING, length, lanes), BF),
            pltpu.VMEM(ln_gain.shape, F32),
            pltpu.VMEM(tokens.shape, BF),
            pltpu.VMEM((2, width, inner), BF),
            dma,
            dma((seqs,)),
            dma((2,)),
        ],
        flops=2 * seqs * length * width * 2 * inner,
        hbm=(1, 2, 3),
        vmem=51,
    )
    both = along_ring(both)
    values = call(
        functools.partial(values_kernel, seqs),
        [block] * RING,
        [pos, normed, weights],
        [pltpu.VMEM((RING, length, lanes), BF), pltpu.VMEM((width, inner), BF), dma],
        flops=2 * seqs * length * width * inner,
        hbm=(2,),
        vmem=20,
    )
    keys = call(functools.partial(place_kernel, RING), whole, [pos, *both, values[0]], unread=(1 + RING,))
    keys_far = other_core(keys)
    values = along_ring(values)
    chunk = (PLANE, half // PLANE, full)
    term = call(
        logits_kernel,
        jax.ShapeDtypeStruct(chunk, BF),
        [pos, *both, keys, keys_far],
        [pltpu.VMEM(whole.shape, BF), pltpu.VMEM(chunk, BF), dma((CORE,))],
        flops=2 * half * full * W * lanes,
        out_specs=HBM,
    )
    terms = lax.all_to_all(term, ("x", "y"), 0, 0, tiled=True)
    probs = call(
        functools.partial(probs_kernel, scale),
        jax.ShapeDtypeStruct(chunk[1:], BF),
        [terms, *values[1:EARLY]],
        unread=range(1, EARLY),
    )
    values = call(functools.partial(place_kernel, RING), whole, [pos, *values])
    values_far = other_core(values)
    rows = call(
        rows_kernel,
        jax.ShapeDtypeStruct((X, *chunk[1:]), BF),
        [pos, *(along(probs, "x", X, s) for s in X_STEPS)],
    ).reshape(length, full)
    context = []
    for step in Y_STEPS:
        near, far = call(
            functools.partial(context_kernel, step),
            [block] * 2,
            [pos, along(rows, "y", Y, step), values, values_far],
            [pltpu.VMEM((W, length, lanes), BF)],
            flops=2 * length * full * W * lanes,
        )
        context += [to_block(near, step, 0), to_block(far, step, Z)]
    return call(
        mix_kernel,
        jax.ShapeDtypeStruct((seqs, length, width), F32),
        [pos, w_out, *context],
        [pltpu.VMEM(w_out.shape, BF), pltpu.VMEM((seqs, length, width), F32), dma((seqs,))],
        flops=2 * seqs * length * inner * width,
        out_specs=HBM,
    )


def solution(mesh):
    cut = Mesh(mesh.devices.reshape(Z, CORE, X, Y, W), ("z", "c", "x", "y", "w"))
    split = P(("x", "y", "w"), ("z", "c"), None)
    return jax.shard_map(shards, mesh=cut, in_specs=(split, P(), P(), P()), out_specs=split, check_vma=False)
```

```python
import functools
import math

import jax
import jax.numpy as jnp
from jax import lax
from jax.experimental import pallas as pl
from jax.experimental.pallas import tpu as pltpu
from jax.sharding import Mesh
from jax.sharding import PartitionSpec as P

HEAD_DIM = 64
Z, CORE, X, Y, W = 4, 2, 4, 4, 2
RING = Z * W
PLANE = X * Y
STEPS = (0, 4, 3, 5, 2, 6, 1, 7)
BF = jnp.bfloat16
F32 = jnp.float32
VMEM = pl.BlockSpec(memory_space=pltpu.VMEM)
HBM = pl.BlockSpec(memory_space=pltpu.HBM)
ANY = pl.BlockSpec(memory_space=pl.ANY)
SMEM = pl.BlockSpec(memory_space=pltpu.SMEM)
CUTS = 4
MIB = 1024 * 1024


def place(index):
    return (index % W) * Z + index // W


def index_of(position):
    return (position % Z) * W + position // Z


def head_at(position):
    pos = lax.rem(position, RING)
    return lax.rem(pos, Z) * W + lax.div(pos, Z)


def blocks_by_head(y, seqs, mine):
    length = y.shape[0] // seqs
    for h in range(mine.shape[0]):
        mine[h] = jnp.concatenate(
            [y[r * length : (r + 1) * length, h * HEAD_DIM : (h + 1) * HEAD_DIM] for r in range(seqs)], axis=1
        ).astype(BF)


def keys_queries_kernel(pos_ref, gain_hbm, x_hbm, w_hbm, *refs):
    both, (normed, mine, gain_ref, x_ref, w_ref, gain_sem, x_sem, w_sem) = refs[:RING], refs[RING:]
    seqs, length, width = x_hbm.shape
    x_copies = [pltpu.make_async_copy(x_hbm.at[r], x_ref.at[r], x_sem.at[r]) for r in range(seqs)]
    w_copies = [
        [pltpu.make_async_copy(w_hbm.at[c, part], w_ref.at[c, part], w_sem.at[c, i]) for i, part in enumerate(cuts(width, CUTS))]
        for c in range(2)
    ]
    gain_copy = pltpu.make_async_copy(gain_hbm, gain_ref, gain_sem)
    for copy in (x_copies[0], gain_copy, *x_copies[1:], *w_copies[1], *w_copies[0]):
        copy.start()
    gain_copy.wait()
    gain = gain_ref[...].reshape(1, width)
    for r in range(seqs):
        x_copies[r].wait()
        x = x_ref[r].astype(F32)
        mean = jnp.mean(x, axis=-1, keepdims=True)
        off = x - mean
        var = jnp.mean(off * off, axis=-1, keepdims=True)
        normed[r * length : (r + 1) * length] = (off / jnp.sqrt(var + 1e-05) * gain).astype(BF)
    pos = pos_ref[0]
    for c in (1, 0):
        for copy in w_copies[c]:
            copy.wait()
        blocks_by_head(jnp.dot(normed[...], w_ref[c], preferred_element_type=F32), seqs, mine)
        for i, s in enumerate(STEPS):
            both[i][(1 - c) * length : (2 - c) * length] = mine[head_at(pos + s)]


def values_kernel(seqs, pos_ref, normed, w_hbm, *refs):
    outs, (mine, w_ref, w_sem) = refs[:RING], refs[RING:]
    copy = pltpu.make_async_copy(w_hbm.at[2], w_ref, w_sem)
    copy.start()
    copy.wait()
    blocks_by_head(jnp.dot(normed[...], w_ref[...], preferred_element_type=F32), seqs, mine)
    pos = pos_ref[0]
    for i, s in enumerate(STEPS):
        outs[i][...] = mine[head_at(pos + s)]


def cuts(rows, count):
    return [pl.ds(i * (rows // count), rows // count) for i in range(count)]


def put_by_sender(pos, parts, first, out):
    length = out.shape[2]
    for part, s in zip(parts, STEPS):
        src = lax.rem(pos + RING - s, RING)
        out[lax.div(src, Z), lax.rem(src, Z)] = part[first : first + length]


def place_kernel(count, pos_ref, *refs):
    put_by_sender(pos_ref[0], refs[:count], 0, refs[-1])


def half_terms(q, keys, side, out_hbm, terms, sem):
    length = keys.shape[2]
    half = keys.shape[1] * length
    columns = pl.ds(side * half, half)
    total = None
    for w in range(W):
        term = lax.dot_general(
            q[w].reshape(half, -1), keys[w].reshape(half, -1), (((1,), (1,)), ((), ())), preferred_element_type=F32
        )
        total = term if total is None else total + term
    copies = []
    for i, rows in enumerate(cuts(half, Z)):
        terms[rows] = total[i * length : (i + 1) * length].astype(BF)
        copies.append(pltpu.make_async_copy(terms.at[rows], out_hbm.at[rows, columns], sem.at[i]))
        copies[i].start()
    for copy in copies:
        copy.wait()


def near_kernel(pos_ref, *refs):
    parts, (k_ref, out_hbm, q, terms, sem) = refs[:RING], refs[RING:]
    put_by_sender(pos_ref[0], parts, q.shape[2], q)
    half_terms(q, k_ref, 0, out_hbm, terms, sem)


def far_kernel(_, q, k_far, out_hbm, terms, sem):
    half_terms(q, k_far, 1, out_hbm, terms, sem)


def probs_kernel(scale, x_ref, *refs):
    out_hbm, probs, sem = refs[-3:]
    logits = x_ref[0].astype(F32)
    for i in range(1, x_ref.shape[0]):
        logits = logits + x_ref[i].astype(F32)
    expo = jnp.exp(logits * scale)
    probs[...] = (expo / jnp.sum(expo, axis=-1, keepdims=True)).astype(BF)
    copies = [pltpu.make_async_copy(probs, out_hbm.at[i], sem.at[i]) for i in range(PLANE)]
    for copy in copies:
        copy.start()
    for copy in copies:
        copy.wait()


def context_kernel(pos_ref, p_ref, v_ref, v_far, *refs):
    outs, mine = refs[:RING], refs[RING]
    half = v_ref.shape[1] * v_ref.shape[2]
    length = v_ref.shape[2]
    for w in range(W):
        a = jnp.dot(p_ref[:, :half], v_ref[w].reshape(half, -1), preferred_element_type=F32)
        a = a + jnp.dot(p_ref[:, half:], v_far[w].reshape(half, -1), preferred_element_type=F32)
        a = a.astype(BF)
        for z in range(Z):
            mine[w * Z + z] = a[z * length : (z + 1) * length]
    pos = pos_ref[0]
    for i, s in enumerate(STEPS):
        outs[i][...] = mine[lax.rem(pos + s, RING)]


def mix_kernel(pos_ref, w_ref, *refs):
    parts, (out_hbm, rows, mixed, sem) = refs[:RING], refs[RING:]
    pos = pos_ref[0]
    for i, s in enumerate(STEPS):
        h = head_at(pos + RING - s)
        rows[i * HEAD_DIM : (i + 1) * HEAD_DIM] = w_ref[pl.ds(pl.multiple_of(h * HEAD_DIM, HEAD_DIM), HEAD_DIM)]
    copies = []
    for r in range(mixed.shape[0]):
        lhs = jnp.concatenate([part[:, r * HEAD_DIM : (r + 1) * HEAD_DIM] for part in parts], axis=1)
        mixed[r] = jnp.dot(lhs, rows[...], preferred_element_type=F32)
        for i, part in enumerate(cuts(mixed.shape[1], CUTS)):
            copies.append(pltpu.make_async_copy(mixed.at[r, part], out_hbm.at[r, part], sem.at[r, i]))
            copies[-1].start()
    for copy in copies:
        copy.wait()


def call(kernel, out_shape, operands, scratch=(), flops=0, hbm=(), unread=(), out_specs=None, aliases=None, vmem=20):
    moved = sum(math.prod(o.shape) * o.dtype.itemsize for o in operands)
    specs = [
        SMEM if o.dtype == jnp.int32 else HBM if i in hbm else ANY if i in unread else VMEM for i, o in enumerate(operands)
    ]
    return pl.pallas_call(
        kernel,
        out_shape=out_shape,
        in_specs=specs,
        out_specs=out_specs or jax.tree.map(lambda _: VMEM, out_shape),
        scratch_shapes=list(scratch),
        input_output_aliases=aliases or {},
        compiler_params=pltpu.CompilerParams(vmem_limit_bytes=vmem * MIB),
        cost_estimate=pl.CostEstimate(flops=flops, bytes_accessed=2 * moved, transcendentals=0),
    )(*operands)


def along_ring(parts):
    got = []
    for part, s in zip(parts, STEPS):
        pairs = [(i, index_of((place(i) + s) % RING)) for i in range(RING)]
        got.append(lax.ppermute(part, ("z", "w"), pairs) if s else part)
    return got


def other_core(a):
    return lax.ppermute(a, "c", [(0, 1), (1, 0)])


def shards(tokens, ln_gain, w_qkv, w_out):
    seqs, length, width = tokens.shape
    inner = w_qkv.shape[2]
    lanes = seqs * HEAD_DIM
    pos = (lax.axis_index("w") * Z + lax.axis_index("z")).astype(jnp.int32).reshape(1)
    pair = jax.ShapeDtypeStruct((2 * length, lanes), BF)
    block = jax.ShapeDtypeStruct((length, lanes), BF)
    whole = jax.ShapeDtypeStruct((W, Z, length, lanes), BF)
    half = Z * length
    full = CORE * half
    scale = 1.0 / math.sqrt(HEAD_DIM * seqs * W * PLANE)

    weights = jnp.transpose(w_qkv, (1, 0, 2))
    dma = pltpu.SemaphoreType.DMA
    *both, normed = call(
        keys_queries_kernel,
        [pair] * RING + [jax.ShapeDtypeStruct((seqs * length, width), BF)],
        [pos, ln_gain, tokens, weights],
        [
            pltpu.VMEM((RING, length, lanes), BF),
            pltpu.VMEM(ln_gain.shape, F32),
            pltpu.VMEM(tokens.shape, BF),
            pltpu.VMEM((2, width, inner), BF),
            dma,
            dma((seqs,)),
            dma((2, CUTS)),
        ],
        flops=2 * seqs * length * width * 2 * inner,
        hbm=(1, 2, 3),
        vmem=51,
    )
    both = along_ring(both)
    values = call(
        functools.partial(values_kernel, seqs),
        [block] * RING,
        [pos, normed, weights],
        [pltpu.VMEM((RING, length, lanes), BF), pltpu.VMEM((width, inner), BF), dma],
        flops=2 * seqs * length * width * inner,
        hbm=(2,),
        vmem=20,
    )
    keys = call(functools.partial(place_kernel, RING), whole, [pos, *both, values[0]], unread=(1 + RING,))
    keys_far = other_core(keys)
    values = along_ring(values)
    term, query = call(
        near_kernel,
        [jax.ShapeDtypeStruct((half, full), BF), whole],
        [pos, *both, keys],
        [pltpu.VMEM((half, half), BF), dma((Z,))],
        flops=2 * half * half * W * lanes,
        out_specs=[HBM, VMEM],
    )
    term = call(
        far_kernel,
        jax.ShapeDtypeStruct((half, full), BF),
        [term, query, keys_far],
        [pltpu.VMEM((half, half), BF), dma((Z,))],
        flops=2 * half * half * W * lanes,
        hbm=(0,),
        out_specs=HBM,
        aliases={0: 0},
    )
    chunk = (PLANE, half // PLANE, full)
    terms = lax.all_to_all(term.reshape(chunk), ("x", "y"), 0, 0, tiled=True)
    early = values[1:5]
    probs = call(
        functools.partial(probs_kernel, scale),
        jax.ShapeDtypeStruct(chunk, BF),
        [terms, *early],
        [pltpu.VMEM(chunk[1:], BF), dma((PLANE,))],
        unread=range(1, 5),
        out_specs=HBM,
    )
    probs = lax.all_to_all(probs, ("x", "y"), 0, 0, tiled=True).reshape(half, full)
    values = call(functools.partial(place_kernel, RING), whole, [pos, *values])
    values_far = other_core(values)
    context = call(
        context_kernel,
        [block] * RING,
        [pos, probs, values, values_far],
        [pltpu.VMEM((RING, length, lanes), BF)],
        flops=2 * half * full * W * lanes,
    )
    context = along_ring(context)
    return call(
        mix_kernel,
        jax.ShapeDtypeStruct((seqs, length, width), F32),
        [pos, w_out, *context],
        [pltpu.VMEM(w_out.shape, BF), pltpu.VMEM((seqs, length, width), F32), dma((seqs, CUTS))],
        flops=2 * seqs * length * inner * width,
        out_specs=HBM,
    )


def solution(mesh):
    cut = Mesh(mesh.devices.reshape(Z, CORE, X, Y, W), ("z", "c", "x", "y", "w"))
    split = P(("x", "y", "w"), ("z", "c"), None)
    return jax.shard_map(shards, mesh=cut, in_specs=(split, P(), P(), P()), out_specs=split, check_vma=False)
```

```python
import functools
import math

import jax
import jax.numpy as jnp
from jax import lax
from jax.experimental import pallas as pl
from jax.experimental.pallas import tpu as pltpu
from jax.sharding import Mesh
from jax.sharding import PartitionSpec as P

HEAD_DIM = 64
Z, CORE, X, Y, W = 4, 2, 4, 4, 2
RING = Z * W
PLANE = X * Y
STEPS = (0, 4, 3, 5, 2, 6, 1, 7)
BF = jnp.bfloat16
F32 = jnp.float32
VMEM = pl.BlockSpec(memory_space=pltpu.VMEM)
HBM = pl.BlockSpec(memory_space=pltpu.HBM)
ANY = pl.BlockSpec(memory_space=pl.ANY)
SMEM = pl.BlockSpec(memory_space=pltpu.SMEM)
LINE = 4
LINE_STEPS = (0, 2, 1, 3)
CUTS = 4
MIB = 1024 * 1024


def place(index):
    return (index % W) * Z + index // W


def index_of(position):
    return (position % Z) * W + position // Z


def head_at(position):
    pos = lax.rem(position, RING)
    return lax.rem(pos, Z) * W + lax.div(pos, Z)


def blocks_by_head(y, seqs, mine):
    length = y.shape[0] // seqs
    for h in range(mine.shape[0]):
        mine[h] = jnp.concatenate(
            [y[r * length : (r + 1) * length, h * HEAD_DIM : (h + 1) * HEAD_DIM] for r in range(seqs)], axis=1
        ).astype(BF)


def keys_queries_kernel(pos_ref, gain_hbm, x_hbm, w_hbm, *refs):
    both, (normed, mine, gain_ref, x_ref, w_ref, gain_sem, x_sem, w_sem) = refs[:RING], refs[RING:]
    seqs, length, width = x_hbm.shape
    x_copies = [pltpu.make_async_copy(x_hbm.at[r], x_ref.at[r], x_sem.at[r]) for r in range(seqs)]
    w_copies = [
        [pltpu.make_async_copy(w_hbm.at[c, part], w_ref.at[c, part], w_sem.at[c, i]) for i, part in enumerate(cuts(width, CUTS))]
        for c in range(2)
    ]
    gain_copy = pltpu.make_async_copy(gain_hbm, gain_ref, gain_sem)
    for copy in (x_copies[0], gain_copy, *x_copies[1:], *w_copies[1], *w_copies[0]):
        copy.start()
    gain_copy.wait()
    gain = gain_ref[...].reshape(1, width)
    for r in range(seqs):
        x_copies[r].wait()
        x = x_ref[r].astype(F32)
        mean = jnp.mean(x, axis=-1, keepdims=True)
        off = x - mean
        var = jnp.mean(off * off, axis=-1, keepdims=True)
        normed[r * length : (r + 1) * length] = (off / jnp.sqrt(var + 1e-05) * gain).astype(BF)
    pos = pos_ref[0]
    for c in (1, 0):
        for copy in w_copies[c]:
            copy.wait()
        blocks_by_head(jnp.dot(normed[...], w_ref[c], preferred_element_type=F32), seqs, mine)
        for i, s in enumerate(STEPS):
            both[i][(1 - c) * length : (2 - c) * length] = mine[head_at(pos + s)]


def values_kernel(seqs, normed, w_hbm, out_ref, w_ref, w_sem):
    copy = pltpu.make_async_copy(w_hbm.at[2], w_ref, w_sem)
    copy.start()
    copy.wait()
    blocks_by_head(jnp.dot(normed[...], w_ref[...], preferred_element_type=F32), seqs, out_ref)


def cuts(rows, count):
    return [pl.ds(i * (rows // count), rows // count) for i in range(count)]


def put_by_sender(pos, parts, first, out):
    length = out.shape[2]
    for part, s in zip(parts, STEPS):
        src = lax.rem(pos + RING - s, RING)
        out[lax.div(src, Z), lax.rem(src, Z)] = part[first : first + length]


def place_kernel(count, pos_ref, *refs):
    put_by_sender(pos_ref[0], refs[:count], 0, refs[-1])


def logits_kernel(pos_ref, *refs):
    parts, k_ref, k_far = refs[:RING], refs[RING], refs[RING + 1]
    outs, q = refs[RING + 2 : -1], refs[-1]
    rows = q.shape[2]
    length = k_ref.shape[2]
    half = k_ref.shape[1] * length
    for part, s in zip(parts, STEPS):
        run = lax.div(lax.rem(pos_ref[0] + RING - s, RING), Z)
        block = -s % Z
        side = block * 2 // Z
        for i in range(length // rows):
            chunk = block * length // rows + i - side * LINE
            slot = lax.rem(chunk + LINE - pos_ref[1 + side], LINE)
            q[run, side * LINE + slot] = part[length + i * rows : length + (i + 1) * rows]
    for core, keys in enumerate((k_ref, k_far)):
        total = None
        for w in range(W):
            term = lax.dot_general(
                q[w].reshape(half, -1), keys[w].reshape(half, -1), (((1,), (1,)), ((), ())), preferred_element_type=F32
            )
            total = term if total is None else total + term
        total = total.astype(BF)
        for i, out in enumerate(outs):
            out[:, core * half : (core + 1) * half] = total[i * rows : (i + 1) * rows]


def added(parts):
    total = parts[0][...].astype(F32)
    for part in parts[1:]:
        total = total + part[...].astype(F32)
    return total


def sum_kernel(*refs):
    for side in range(2):
        refs[2 * LINE + side][...] = added(refs[side * LINE : (side + 1) * LINE]).astype(BF)


def probs_kernel(scale, *refs):
    for side in range(2):
        expo = jnp.exp(added(refs[side * LINE : (side + 1) * LINE]) * scale)
        refs[side - 2][...] = (expo / jnp.sum(expo, axis=-1, keepdims=True)).astype(BF)


def context_kernel(pos_ref, *refs):
    parts, v_ref, v_far = refs[: 2 * LINE], refs[2 * LINE], refs[2 * LINE + 1]
    outs, (probs, mine) = refs[2 * LINE + 2 : -2], refs[-2:]
    for side in range(2):
        for part, s in zip(parts[side * LINE : (side + 1) * LINE], LINE_STEPS):
            probs[side * LINE + lax.rem(pos_ref[1 + side] + LINE - s, LINE)] = part[...]
    length = v_ref.shape[1]
    half = Z * length
    p = probs[...].reshape(half, -1)
    for w in range(W):
        near, far = (jnp.concatenate([v[z * W + w] for z in range(Z)], axis=0) for v in (v_ref, v_far))
        a = jnp.dot(p[:, :half], near, preferred_element_type=F32)
        a = a + jnp.dot(p[:, half:], far, preferred_element_type=F32)
        mine[w] = a.astype(BF).reshape(mine.shape[1:])
    for i, s in enumerate(STEPS):
        outs[i][...] = mine[lax.div(lax.rem(pos_ref[0] + s, RING), Z), s % Z]


def mix_kernel(pos_ref, w_ref, *refs):
    parts, (out_hbm, rows, mixed, sem) = refs[:RING], refs[RING:]
    pos = pos_ref[0]
    for i, s in enumerate(STEPS):
        h = head_at(pos + RING - s)
        rows[i * HEAD_DIM : (i + 1) * HEAD_DIM] = w_ref[pl.ds(pl.multiple_of(h * HEAD_DIM, HEAD_DIM), HEAD_DIM)]
    copies = []
    for r in range(mixed.shape[0]):
        lhs = jnp.concatenate([part[:, r * HEAD_DIM : (r + 1) * HEAD_DIM] for part in parts], axis=1)
        mixed[r] = jnp.dot(lhs, rows[...], preferred_element_type=F32)
        for i, part in enumerate(cuts(mixed.shape[1], CUTS)):
            copies.append(pltpu.make_async_copy(mixed.at[r, part], out_hbm.at[r, part], sem.at[r, i]))
            copies[-1].start()
    for copy in copies:
        copy.wait()


def call(kernel, out_shape, operands, scratch=(), flops=0, hbm=(), unread=(), out_specs=None, aliases=None, vmem=20):
    moved = sum(math.prod(o.shape) * o.dtype.itemsize for o in operands)
    specs = [
        SMEM if o.dtype == jnp.int32 else HBM if i in hbm else ANY if i in unread else VMEM for i, o in enumerate(operands)
    ]
    return pl.pallas_call(
        kernel,
        out_shape=out_shape,
        in_specs=specs,
        out_specs=out_specs or jax.tree.map(lambda _: VMEM, out_shape),
        scratch_shapes=list(scratch),
        input_output_aliases=aliases or {},
        compiler_params=pltpu.CompilerParams(vmem_limit_bytes=vmem * MIB),
        cost_estimate=pl.CostEstimate(flops=flops, bytes_accessed=2 * moved, transcendentals=0),
    )(*operands)


def along_ring(parts):
    got = []
    for part, s in zip(parts, STEPS):
        pairs = [(i, index_of((place(i) + s) % RING)) for i in range(RING)]
        got.append(lax.ppermute(part, ("z", "w"), pairs) if s else part)
    return got


def along_line(parts, axis):
    return [
        lax.ppermute(part, axis, [(i, (i + s) % LINE) for i in range(LINE)]) if s else part
        for part, s in zip(parts, LINE_STEPS)
    ]


def other_core(a):
    return lax.ppermute(a, "c", [(0, 1), (1, 0)])


def shards(tokens, ln_gain, w_qkv, w_out):
    seqs, length, width = tokens.shape
    inner = w_qkv.shape[2]
    lanes = seqs * HEAD_DIM
    ring = lax.axis_index("w") * Z + lax.axis_index("z")
    pos = jnp.stack([ring, lax.axis_index("x"), lax.axis_index("y")]).astype(jnp.int32)
    pair = jax.ShapeDtypeStruct((2 * length, lanes), BF)
    block = jax.ShapeDtypeStruct((length, lanes), BF)
    whole = jax.ShapeDtypeStruct((W, Z, length, lanes), BF)
    half = Z * length
    full = CORE * half
    scale = 1.0 / math.sqrt(HEAD_DIM * seqs * W * PLANE)

    weights = jnp.transpose(w_qkv, (1, 0, 2))
    dma = pltpu.SemaphoreType.DMA
    *both, normed = call(
        keys_queries_kernel,
        [pair] * RING + [jax.ShapeDtypeStruct((seqs * length, width), BF)],
        [pos, ln_gain, tokens, weights],
        [
            pltpu.VMEM((RING, length, lanes), BF),
            pltpu.VMEM(ln_gain.shape, F32),
            pltpu.VMEM(tokens.shape, BF),
            pltpu.VMEM((2, width, inner), BF),
            dma,
            dma((seqs,)),
            dma((2, CUTS)),
        ],
        flops=2 * seqs * length * width * 2 * inner,
        hbm=(1, 2, 3),
        vmem=51,
    )
    both = along_ring(both)
    values = call(
        functools.partial(values_kernel, seqs),
        jax.ShapeDtypeStruct((RING, length, lanes), BF),
        [normed, weights],
        [pltpu.VMEM((width, inner), BF), dma],
        flops=2 * seqs * length * width * inner,
        hbm=(1,),
    )
    keys = call(functools.partial(place_kernel, RING), whole, [pos, *both, values], unread=(1 + RING,))
    keys_far = other_core(keys)
    values = lax.all_to_all(values, ("z", "w"), 0, 0, tiled=True)
    strip = jax.ShapeDtypeStruct((half // (2 * LINE), full), BF)
    terms = call(
        logits_kernel,
        [strip] * (2 * LINE),
        [pos, *both, keys, keys_far],
        [pltpu.VMEM((W, 2 * LINE, strip.shape[0], lanes), BF)],
        flops=2 * half * full * W * lanes,
    )
    by_x = along_line([terms[s] for s in LINE_STEPS], "x")
    by_y = along_line([terms[LINE + s] for s in LINE_STEPS], "y")
    by_x, by_y = call(sum_kernel, [strip] * 2, [*by_x, *by_y])
    by_x = along_line([by_x] * LINE, "y")
    by_y = along_line([by_y] * LINE, "x")
    by_x, by_y = call(
        functools.partial(probs_kernel, scale), [strip] * 2, [*by_x, *by_y, values], unread=(2 * LINE,)
    )
    by_x = along_line([by_x] * LINE, "x")
    by_y = along_line([by_y] * LINE, "y")
    values_far = other_core(values)
    context = call(
        context_kernel,
        [block] * RING,
        [pos, *by_x, *by_y, values, values_far],
        [pltpu.VMEM((2 * LINE, *strip.shape), BF), pltpu.VMEM(whole.shape, BF)],
        flops=2 * half * full * W * lanes,
    )
    context = along_ring(context)
    return call(
        mix_kernel,
        jax.ShapeDtypeStruct((seqs, length, width), F32),
        [pos, w_out, *context],
        [pltpu.VMEM(w_out.shape, BF), pltpu.VMEM((seqs, length, width), F32), dma((seqs, CUTS))],
        flops=2 * seqs * length * inner * width,
        out_specs=HBM,
    )


def solution(mesh):
    cut = Mesh(mesh.devices.reshape(Z, CORE, X, Y, W), ("z", "c", "x", "y", "w"))
    split = P(("x", "y", "w"), ("z", "c"), None)
    return jax.shard_map(shards, mesh=cut, in_specs=(split, P(), P(), P()), out_specs=split, check_vma=False)
```

```python
import functools
import math

import jax
import jax.numpy as jnp
from jax import lax
from jax.experimental import pallas as pl
from jax.experimental.pallas import tpu as pltpu
from jax.sharding import Mesh
from jax.sharding import PartitionSpec as P

HEAD_DIM = 64
Z, CORE, X, Y, W = 4, 2, 4, 4, 2
RING = Z * W
PLANE = X * Y
STEPS = (0, 4, 3, 5, 2, 6, 1, 7)
BF = jnp.bfloat16
F32 = jnp.float32
VMEM = pl.BlockSpec(memory_space=pltpu.VMEM)
HBM = pl.BlockSpec(memory_space=pltpu.HBM)
ANY = pl.BlockSpec(memory_space=pl.ANY)
SMEM = pl.BlockSpec(memory_space=pltpu.SMEM)
CONTEXT_STEPS = (0, 4, 3, 7, 5, 2, 6, 1)
MIB = 1024 * 1024


def place(index):
    return (index % W) * Z + index // W


def index_of(position):
    return (position % Z) * W + position // Z


def head_at(position):
    pos = lax.rem(position, RING)
    return lax.rem(pos, Z) * W + lax.div(pos, Z)


def blocks_by_head(y, seqs, mine):
    length = y.shape[0] // seqs
    for h in range(mine.shape[0]):
        mine[h] = jnp.concatenate(
            [y[r * length : (r + 1) * length, h * HEAD_DIM : (h + 1) * HEAD_DIM] for r in range(seqs)], axis=1
        ).astype(BF)


def keys_queries_kernel(pos_ref, gain_hbm, x_hbm, w_hbm, *refs):
    both, (normed, mine, gain_ref, x_ref, w_ref, gain_sem, x_sem, w_sem) = refs[:RING], refs[RING:]
    seqs, length, width = x_hbm.shape
    x_copies = [pltpu.make_async_copy(x_hbm.at[r], x_ref.at[r], x_sem.at[r]) for r in range(seqs)]
    w_copies = [pltpu.make_async_copy(w_hbm.at[c], w_ref.at[c], w_sem.at[c]) for c in range(2)]
    gain_copy = pltpu.make_async_copy(gain_hbm, gain_ref, gain_sem)
    for copy in (x_copies[0], gain_copy, *x_copies[1:], w_copies[1], w_copies[0]):
        copy.start()
    gain_copy.wait()
    gain = gain_ref[...].reshape(1, width)
    for r in range(seqs):
        x_copies[r].wait()
        x = x_ref[r].astype(F32)
        mean = jnp.mean(x, axis=-1, keepdims=True)
        off = x - mean
        var = jnp.mean(off * off, axis=-1, keepdims=True)
        normed[r * length : (r + 1) * length] = (off / jnp.sqrt(var + 1e-05) * gain).astype(BF)
    pos = pos_ref[0]
    for c in (1, 0):
        w_copies[c].wait()
        blocks_by_head(jnp.dot(normed[...], w_ref[c], preferred_element_type=F32), seqs, mine)
        for i, s in enumerate(STEPS):
            both[i][(1 - c) * length : (2 - c) * length] = mine[head_at(pos + s)]


def values_kernel(seqs, pos_ref, normed, w_hbm, *refs):
    outs, (mine, w_ref, w_sem) = refs[:RING], refs[RING:]
    copy = pltpu.make_async_copy(w_hbm.at[2], w_ref, w_sem)
    copy.start()
    copy.wait()
    blocks_by_head(jnp.dot(normed[...], w_ref[...], preferred_element_type=F32), seqs, mine)
    pos = pos_ref[0]
    for i, s in enumerate(STEPS):
        outs[i][...] = mine[head_at(pos + s)]


def cuts(rows, count):
    return [pl.ds(i * (rows // count), rows // count) for i in range(count)]


def put_by_sender(pos, parts, first, out):
    length = out.shape[2]
    for part, s in zip(parts, STEPS):
        src = lax.rem(pos + RING - s, RING)
        out[lax.div(src, Z), -s % Z] = part[first : first + length]


def place_kernel(count, pos_ref, *refs):
    put_by_sender(pos_ref[0], refs[:count], 0, refs[-1])


def half_terms(q, keys, side, out_hbm, terms, sem):
    length = keys.shape[2]
    half = keys.shape[1] * length
    columns = pl.ds(side * half, half)
    total = None
    for w in range(W):
        term = lax.dot_general(
            q[w].reshape(half, -1), keys[w].reshape(half, -1), (((1,), (1,)), ((), ())), preferred_element_type=F32
        )
        total = term if total is None else total + term
    copies = []
    for i, rows in enumerate(cuts(half, Z)):
        terms[rows] = total[i * length : (i + 1) * length].astype(BF)
        copies.append(pltpu.make_async_copy(terms.at[rows], out_hbm.at[rows, columns], sem.at[i]))
        copies[i].start()
    for copy in copies:
        copy.wait()


def near_kernel(pos_ref, *refs):
    parts, (k_ref, out_hbm, q, terms, sem) = refs[:RING], refs[RING:]
    put_by_sender(pos_ref[0], parts, q.shape[2], q)
    half_terms(q, k_ref, 0, out_hbm, terms, sem)


def far_kernel(_, q, k_far, out_hbm, terms, sem):
    half_terms(q, k_far, 1, out_hbm, terms, sem)


def probs_kernel(scale, x_ref, *refs):
    out_hbm, probs, sem = refs[-3:]
    logits = x_ref[0].astype(F32)
    for i in range(1, x_ref.shape[0]):
        logits = logits + x_ref[i].astype(F32)
    expo = jnp.exp(logits * scale)
    probs[...] = (expo / jnp.sum(expo, axis=-1, keepdims=True)).astype(BF)
    copies = [pltpu.make_async_copy(probs, out_hbm.at[i], sem.at[i]) for i in range(PLANE)]
    for copy in copies:
        copy.start()
    for copy in copies:
        copy.wait()


def seen_kernel(_, out_ref):
    out_ref[...] = jnp.zeros_like(out_ref)


def context_kernel(blocks, steps, pos_ref, p_ref, v_ref, v_far, _, *refs):
    outs, mine = refs[: len(steps)], refs[-1]
    half = v_ref.shape[1] * v_ref.shape[2]
    length = v_ref.shape[2]
    p = jnp.concatenate([p_ref[t * length : (t + 1) * length] for t in blocks], axis=0)
    for w in range(W):
        a = jnp.dot(p[:, :half], v_ref[w].reshape(half, -1), preferred_element_type=F32)
        a = a + jnp.dot(p[:, half:], v_far[w].reshape(half, -1), preferred_element_type=F32)
        mine[w] = a.astype(BF).reshape(mine.shape[1:])
    for out, s in zip(outs, steps):
        out[...] = mine[lax.div(lax.rem(pos_ref[0] + s, RING), Z), blocks.index(s % Z)]


def mix_kernel(pos_ref, w_ref, *refs):
    parts, (out_hbm, rows, mixed, sem) = refs[:RING], refs[RING:]
    pos = pos_ref[0]
    for i, s in enumerate(CONTEXT_STEPS):
        h = head_at(pos + RING - s)
        rows[i * HEAD_DIM : (i + 1) * HEAD_DIM] = w_ref[pl.ds(pl.multiple_of(h * HEAD_DIM, HEAD_DIM), HEAD_DIM)]
    copies = []
    for r in range(mixed.shape[0]):
        lhs = jnp.concatenate([part[:, r * HEAD_DIM : (r + 1) * HEAD_DIM] for part in parts], axis=1)
        mixed[r] = jnp.dot(lhs, rows[...], preferred_element_type=F32)
        copies.append(pltpu.make_async_copy(mixed.at[r], out_hbm.at[r], sem.at[r]))
        copies[r].start()
    for copy in copies:
        copy.wait()


def call(kernel, out_shape, operands, scratch=(), flops=0, hbm=(), unread=(), out_specs=None, aliases=None, vmem=20):
    moved = sum(math.prod(o.shape) * o.dtype.itemsize for o in operands)
    specs = [
        SMEM if o.dtype == jnp.int32 else HBM if i in hbm else ANY if i in unread else VMEM for i, o in enumerate(operands)
    ]
    return pl.pallas_call(
        kernel,
        out_shape=out_shape,
        in_specs=specs,
        out_specs=out_specs or jax.tree.map(lambda _: VMEM, out_shape),
        scratch_shapes=list(scratch),
        input_output_aliases=aliases or {},
        compiler_params=pltpu.CompilerParams(vmem_limit_bytes=vmem * MIB),
        cost_estimate=pl.CostEstimate(flops=flops, bytes_accessed=2 * moved, transcendentals=0),
    )(*operands)


def along_ring(parts, steps=STEPS):
    got = []
    for part, s in zip(parts, steps):
        pairs = [(i, index_of((place(i) + s) % RING)) for i in range(RING)]
        got.append(lax.ppermute(part, ("z", "w"), pairs) if s else part)
    return got


def other_core(a):
    return lax.ppermute(a, "c", [(0, 1), (1, 0)])


def shards(tokens, ln_gain, w_qkv, w_out):
    seqs, length, width = tokens.shape
    inner = w_qkv.shape[2]
    lanes = seqs * HEAD_DIM
    pos = (lax.axis_index("w") * Z + lax.axis_index("z")).astype(jnp.int32).reshape(1)
    pair = jax.ShapeDtypeStruct((2 * length, lanes), BF)
    block = jax.ShapeDtypeStruct((length, lanes), BF)
    whole = jax.ShapeDtypeStruct((W, Z, length, lanes), BF)
    half = Z * length
    full = CORE * half
    scale = 1.0 / math.sqrt(HEAD_DIM * seqs * W * PLANE)

    weights = jnp.transpose(w_qkv, (1, 0, 2))
    dma = pltpu.SemaphoreType.DMA
    *both, normed = call(
        keys_queries_kernel,
        [pair] * RING + [jax.ShapeDtypeStruct((seqs * length, width), BF)],
        [pos, ln_gain, tokens, weights],
        [
            pltpu.VMEM((RING, length, lanes), BF),
            pltpu.VMEM(ln_gain.shape, F32),
            pltpu.VMEM(tokens.shape, BF),
            pltpu.VMEM((2, width, inner), BF),
            dma,
            dma((seqs,)),
            dma((2,)),
        ],
        flops=2 * seqs * length * width * 2 * inner,
        hbm=(1, 2, 3),
        vmem=51,
    )
    both = along_ring(both)
    values = call(
        functools.partial(values_kernel, seqs),
        [block] * RING,
        [pos, normed, weights],
        [pltpu.VMEM((RING, length, lanes), BF), pltpu.VMEM((width, inner), BF), dma],
        flops=2 * seqs * length * width * inner,
        hbm=(2,),
        vmem=20,
    )
    keys = call(functools.partial(place_kernel, RING), whole, [pos, *both, values[0]], unread=(1 + RING,))
    keys_far = other_core(keys)
    values = along_ring(values)
    term, query = call(
        near_kernel,
        [jax.ShapeDtypeStruct((half, full), BF), whole],
        [pos, *both, keys],
        [pltpu.VMEM((half, half), BF), dma((Z,))],
        flops=2 * half * half * W * lanes,
        out_specs=[HBM, VMEM],
    )
    term = call(
        far_kernel,
        jax.ShapeDtypeStruct((half, full), BF),
        [term, query, keys_far],
        [pltpu.VMEM((half, half), BF), dma((Z,))],
        flops=2 * half * half * W * lanes,
        hbm=(0,),
        out_specs=HBM,
        aliases={0: 0},
    )
    chunk = (PLANE, half // PLANE, full)
    terms = lax.all_to_all(term.reshape(chunk), ("x", "y"), 0, 0, tiled=True)
    early = values[1:5]
    probs = call(
        functools.partial(probs_kernel, scale),
        jax.ShapeDtypeStruct(chunk, BF),
        [terms, *early],
        [pltpu.VMEM(chunk[1:], BF), dma((PLANE,))],
        unread=range(1, 5),
        out_specs=HBM,
    )
    probs = lax.all_to_all(probs, ("x", "y"), 0, 0, tiled=True).reshape(half, full)
    values = call(functools.partial(place_kernel, RING), whole, [pos, *values])
    values_far = other_core(values)
    seen = call(seen_kernel, jax.ShapeDtypeStruct((8, 128), F32), [values_far], unread=(0,))
    context = []
    for blocks in ((0, 3), (1, 2)):
        steps = [s for s in CONTEXT_STEPS if s % Z in blocks]
        parts = call(
            functools.partial(context_kernel, blocks, steps),
            [block] * len(steps),
            [pos, probs, values, values_far, seen],
            [pltpu.VMEM((W, len(blocks), length, lanes), BF)],
            flops=half * full * W * lanes,
            unread=(4,),
        )
        context += along_ring(parts, steps)
    return call(
        mix_kernel,
        jax.ShapeDtypeStruct((seqs, length, width), F32),
        [pos, w_out, *context],
        [pltpu.VMEM(w_out.shape, BF), pltpu.VMEM((seqs, length, width), F32), dma((seqs,))],
        flops=2 * seqs * length * inner * width,
        out_specs=HBM,
    )


def solution(mesh):
    cut = Mesh(mesh.devices.reshape(Z, CORE, X, Y, W), ("z", "c", "x", "y", "w"))
    split = P(("x", "y", "w"), ("z", "c"), None)
    return jax.shard_map(shards, mesh=cut, in_specs=(split, P(), P(), P()), out_specs=split, check_vma=False)
```

```python
import functools
import math

import jax
import jax.numpy as jnp
from jax import lax
from jax.experimental import pallas as pl
from jax.experimental.pallas import tpu as pltpu
from jax.sharding import Mesh
from jax.sharding import PartitionSpec as P

HEAD_DIM = 64
Z, CORE, X, Y, W = 4, 2, 4, 4, 2
RING = Z * W
PLANE = X * Y
STEPS = (0, 7, 1, 5, 3, 4, 6, 2)
BF = jnp.bfloat16
F32 = jnp.float32
VMEM = pl.BlockSpec(memory_space=pltpu.VMEM)
HBM = pl.BlockSpec(memory_space=pltpu.HBM)
ANY = pl.BlockSpec(memory_space=pl.ANY)
SMEM = pl.BlockSpec(memory_space=pltpu.SMEM)
CONTEXT_STEPS = (0, 4, 3, 7, 5, 2, 6, 1)
MIB = 1024 * 1024


def place(index):
    return (index % W) * Z + index // W


def index_of(position):
    return (position % Z) * W + position // Z


def head_at(position):
    pos = lax.rem(position, RING)
    return lax.rem(pos, Z) * W + lax.div(pos, Z)


def blocks_by_head(y, seqs, mine):
    length = y.shape[0] // seqs
    for h in range(mine.shape[0]):
        mine[h] = jnp.concatenate(
            [y[r * length : (r + 1) * length, h * HEAD_DIM : (h + 1) * HEAD_DIM] for r in range(seqs)], axis=1
        ).astype(BF)


def keys_queries_kernel(pos_ref, gain_hbm, x_hbm, w_hbm, *refs):
    both, (normed, mine, gain_ref, x_ref, w_ref, gain_sem, x_sem, w_sem) = refs[:RING], refs[RING:]
    seqs, length, width = x_hbm.shape
    x_copies = [pltpu.make_async_copy(x_hbm.at[r], x_ref.at[r], x_sem.at[r]) for r in range(seqs)]
    w_copies = [pltpu.make_async_copy(w_hbm.at[c], w_ref.at[c], w_sem.at[c]) for c in range(2)]
    gain_copy = pltpu.make_async_copy(gain_hbm, gain_ref, gain_sem)
    for copy in (x_copies[0], gain_copy, *x_copies[1:], w_copies[1], w_copies[0]):
        copy.start()
    def norm(r):
        x = x_ref[r].astype(F32)
        mean = jnp.mean(x, axis=-1, keepdims=True)
        off = x - mean
        var = jnp.mean(off * off, axis=-1, keepdims=True)
        normed[r * length : (r + 1) * length] = (off / jnp.sqrt(var + 1e-05) * gain).astype(BF)

    def project(c, r):
        y = jnp.dot(normed[r * length : (r + 2) * length], w_ref[c], preferred_element_type=F32)
        for h in range(mine.shape[1]):
            columns = slice(h * HEAD_DIM, (h + 1) * HEAD_DIM)
            block = jnp.concatenate([y[:length, columns], y[length:, columns]], axis=1)
            mine[c, h, :, r * HEAD_DIM : (r + 2) * HEAD_DIM] = block.astype(BF)

    gain_copy.wait()
    gain = gain_ref[...].reshape(1, width)
    for r in range(seqs // 2):
        x_copies[r].wait()
        norm(r)
    for r in range(seqs // 2, seqs):
        x_copies[r].wait()
    w_copies[1].wait()
    for r in range(0, seqs // 2, 2):
        project(1, r)
    for r in range(seqs // 2, seqs):
        norm(r)
    w_copies[0].wait()
    for r in range(0, seqs // 2, 2):
        project(0, r)
    for r in range(seqs // 2, seqs, 2):
        project(1, r)
        project(0, r)
    pos = pos_ref[0]
    for c in (1, 0):
        for i, s in enumerate(STEPS):
            both[i][(1 - c) * length : (2 - c) * length] = mine[c, head_at(pos + s)]


def values_kernel(seqs, pos_ref, normed, w_hbm, *refs):
    outs, (mine, w_ref, w_sem) = refs[:RING], refs[RING:]
    copy = pltpu.make_async_copy(w_hbm.at[2], w_ref, w_sem)
    copy.start()
    copy.wait()
    blocks_by_head(jnp.dot(normed[...], w_ref[...], preferred_element_type=F32), seqs, mine)
    pos = pos_ref[0]
    for i, s in enumerate(STEPS):
        outs[i][...] = mine[head_at(pos + s)]


def cuts(rows, count):
    return [pl.ds(i * (rows // count), rows // count) for i in range(count)]


def put_by_sender(pos, parts, first, out):
    length = out.shape[2]
    for part, s in zip(parts, STEPS):
        src = lax.rem(pos + RING - s, RING)
        out[lax.div(src, Z), -s % Z] = part[first : first + length]


def place_kernel(count, pos_ref, *refs):
    put_by_sender(pos_ref[0], refs[:count], 0, refs[-1])


def half_terms(q, keys, side, out_hbm, terms, sem):
    length = keys.shape[2]
    half = keys.shape[1] * length
    columns = pl.ds(side * half, half)
    copies = []
    for i, rows in enumerate(cuts(half, 2)):
        total = None
        for w in range(W):
            term = lax.dot_general(
                q[w, i * Z // 2 : (i + 1) * Z // 2].reshape(half // 2, -1),
                keys[w].reshape(half, -1),
                (((1,), (1,)), ((), ())),
                preferred_element_type=F32,
            )
            total = term if total is None else total + term
        terms[rows] = total.astype(BF)
        copies.append(pltpu.make_async_copy(terms.at[rows], out_hbm.at[rows, columns], sem.at[i]))
        copies[i].start()
    for copy in copies:
        copy.wait()


def near_kernel(pos_ref, *refs):
    parts, (k_ref, out_hbm, q, terms, sem) = refs[:RING], refs[RING:]
    put_by_sender(pos_ref[0], parts, q.shape[2], q)
    half_terms(q, k_ref, 0, out_hbm, terms, sem)


def far_kernel(_, q, k_far, out_hbm, terms, sem):
    half_terms(q, k_far, 1, out_hbm, terms, sem)


def probs_kernel(scale, x_ref, *refs):
    out_hbm, probs, sem = refs[-3:]
    logits = x_ref[0].astype(F32)
    for i in range(1, x_ref.shape[0]):
        logits = logits + x_ref[i].astype(F32)
    expo = jnp.exp(logits * scale)
    probs[...] = (expo / jnp.sum(expo, axis=-1, keepdims=True)).astype(BF)
    copies = [pltpu.make_async_copy(probs, out_hbm.at[i], sem.at[i]) for i in range(PLANE)]
    for copy in copies:
        copy.start()
    for copy in copies:
        copy.wait()


def seen_kernel(_, out_ref):
    out_ref[...] = jnp.zeros_like(out_ref)


def context_kernel(blocks, steps, pos_ref, p_ref, v_ref, v_far, _, *refs):
    outs, mine = refs[: len(steps)], refs[-1]
    half = v_ref.shape[1] * v_ref.shape[2]
    length = v_ref.shape[2]
    p = jnp.concatenate([p_ref[t * length : (t + 1) * length] for t in blocks], axis=0)
    for w in range(W):
        a = jnp.dot(p[:, :half], v_ref[w].reshape(half, -1), preferred_element_type=F32)
        a = a + jnp.dot(p[:, half:], v_far[w].reshape(half, -1), preferred_element_type=F32)
        mine[w] = a.astype(BF).reshape(mine.shape[1:])
    for out, s in zip(outs, steps):
        out[...] = mine[lax.div(lax.rem(pos_ref[0] + s, RING), Z), blocks.index(s % Z)]


def mix_kernel(pos_ref, w_ref, *refs):
    parts, (out_hbm, rows, mixed, sem) = refs[:RING], refs[RING:]
    pos = pos_ref[0]
    for i, s in enumerate(CONTEXT_STEPS):
        h = head_at(pos + RING - s)
        rows[i * HEAD_DIM : (i + 1) * HEAD_DIM] = w_ref[pl.ds(pl.multiple_of(h * HEAD_DIM, HEAD_DIM), HEAD_DIM)]
    copies = []
    for r in range(mixed.shape[0]):
        lhs = jnp.concatenate([part[:, r * HEAD_DIM : (r + 1) * HEAD_DIM] for part in parts], axis=1)
        mixed[r] = jnp.dot(lhs, rows[...], preferred_element_type=F32)
        copies.append(pltpu.make_async_copy(mixed.at[r], out_hbm.at[r], sem.at[r]))
        copies[r].start()
    for copy in copies:
        copy.wait()


def call(kernel, out_shape, operands, scratch=(), flops=0, hbm=(), unread=(), out_specs=None, aliases=None, vmem=20):
    moved = sum(math.prod(o.shape) * o.dtype.itemsize for o in operands)
    specs = [
        SMEM if o.dtype == jnp.int32 else HBM if i in hbm else ANY if i in unread else VMEM for i, o in enumerate(operands)
    ]
    return pl.pallas_call(
        kernel,
        out_shape=out_shape,
        in_specs=specs,
        out_specs=out_specs or jax.tree.map(lambda _: VMEM, out_shape),
        scratch_shapes=list(scratch),
        input_output_aliases=aliases or {},
        compiler_params=pltpu.CompilerParams(vmem_limit_bytes=vmem * MIB),
        cost_estimate=pl.CostEstimate(flops=flops, bytes_accessed=2 * moved, transcendentals=0),
    )(*operands)


def along_ring(parts, steps=STEPS):
    got = []
    for part, s in zip(parts, steps):
        pairs = [(i, index_of((place(i) + s) % RING)) for i in range(RING)]
        got.append(lax.ppermute(part, ("z", "w"), pairs) if s else part)
    return got


def other_core(a):
    return lax.ppermute(a, "c", [(0, 1), (1, 0)])


def shards(tokens, ln_gain, w_qkv, w_out):
    seqs, length, width = tokens.shape
    inner = w_qkv.shape[2]
    lanes = seqs * HEAD_DIM
    pos = (lax.axis_index("w") * Z + lax.axis_index("z")).astype(jnp.int32).reshape(1)
    pair = jax.ShapeDtypeStruct((2 * length, lanes), BF)
    block = jax.ShapeDtypeStruct((length, lanes), BF)
    whole = jax.ShapeDtypeStruct((W, Z, length, lanes), BF)
    half = Z * length
    full = CORE * half
    scale = 1.0 / math.sqrt(HEAD_DIM * seqs * W * PLANE)

    weights = jnp.transpose(w_qkv, (1, 0, 2))
    dma = pltpu.SemaphoreType.DMA
    *both, normed = call(
        keys_queries_kernel,
        [pair] * RING + [jax.ShapeDtypeStruct((seqs * length, width), BF)],
        [pos, ln_gain, tokens, weights],
        [
            pltpu.VMEM((2, RING, length, lanes), BF),
            pltpu.VMEM(ln_gain.shape, F32),
            pltpu.VMEM(tokens.shape, BF),
            pltpu.VMEM((2, width, inner), BF),
            dma,
            dma((seqs,)),
            dma((2,)),
        ],
        flops=2 * seqs * length * width * 2 * inner,
        hbm=(1, 2, 3),
        vmem=51,
    )
    both = along_ring(both)
    values = call(
        functools.partial(values_kernel, seqs),
        [block] * RING,
        [pos, normed, weights],
        [pltpu.VMEM((RING, length, lanes), BF), pltpu.VMEM((width, inner), BF), dma],
        flops=2 * seqs * length * width * inner,
        hbm=(2,),
        vmem=20,
    )
    keys = call(functools.partial(place_kernel, RING), whole, [pos, *both, values[0]], unread=(1 + RING,))
    keys_far = other_core(keys)
    values = along_ring(values)
    term, query = call(
        near_kernel,
        [jax.ShapeDtypeStruct((half, full), BF), whole],
        [pos, *both, keys],
        [pltpu.VMEM((half, half), BF), dma((2,))],
        flops=2 * half * half * W * lanes,
        out_specs=[HBM, VMEM],
    )
    term = call(
        far_kernel,
        jax.ShapeDtypeStruct((half, full), BF),
        [term, query, keys_far],
        [pltpu.VMEM((half, half), BF), dma((2,))],
        flops=2 * half * half * W * lanes,
        hbm=(0,),
        out_specs=HBM,
        aliases={0: 0},
    )
    chunk = (PLANE, half // PLANE, full)
    terms = lax.all_to_all(term.reshape(chunk), ("x", "y"), 0, 0, tiled=True)
    early = values[1:5]
    probs = call(
        functools.partial(probs_kernel, scale),
        jax.ShapeDtypeStruct(chunk, BF),
        [terms, *early],
        [pltpu.VMEM(chunk[1:], BF), dma((PLANE,))],
        unread=range(1, 5),
        out_specs=HBM,
    )
    probs = lax.all_to_all(probs, ("x", "y"), 0, 0, tiled=True).reshape(half, full)
    values = call(functools.partial(place_kernel, RING), whole, [pos, *values])
    values_far = other_core(values)
    seen = call(seen_kernel, jax.ShapeDtypeStruct((8, 128), F32), [values_far], unread=(0,))
    context = []
    for blocks in ((0, 3), (1, 2)):
        steps = [s for s in CONTEXT_STEPS if s % Z in blocks]
        parts = call(
            functools.partial(context_kernel, blocks, steps),
            [block] * len(steps),
            [pos, probs, values, values_far, seen],
            [pltpu.VMEM((W, len(blocks), length, lanes), BF)],
            flops=half * full * W * lanes,
            unread=(4,),
        )
        context += along_ring(parts, steps)
    return call(
        mix_kernel,
        jax.ShapeDtypeStruct((seqs, length, width), F32),
        [pos, w_out, *context],
        [pltpu.VMEM(w_out.shape, BF), pltpu.VMEM((seqs, length, width), F32), dma((seqs,))],
        flops=2 * seqs * length * inner * width,
        out_specs=HBM,
    )


def solution(mesh):
    cut = Mesh(mesh.devices.reshape(Z, CORE, X, Y, W), ("z", "c", "x", "y", "w"))
    split = P(("x", "y", "w"), ("z", "c"), None)
    return jax.shard_map(shards, mesh=cut, in_specs=(split, P(), P(), P()), out_specs=split, check_vma=False)
```

```python
import functools
import math

import jax
import jax.numpy as jnp
from jax import lax
from jax.experimental import pallas as pl
from jax.experimental.pallas import tpu as pltpu
from jax.sharding import Mesh
from jax.sharding import PartitionSpec as P

HEAD_DIM = 64
Z, CORE, X, Y, W = 4, 2, 4, 4, 2
RING = Z * W
PLANE = X * Y
STEPS = (0, 2, 6, 3, 5, 4, 1, 7)
BF = jnp.bfloat16
F32 = jnp.float32
VMEM = pl.BlockSpec(memory_space=pltpu.VMEM)
HBM = pl.BlockSpec(memory_space=pltpu.HBM)
ANY = pl.BlockSpec(memory_space=pl.ANY)
SMEM = pl.BlockSpec(memory_space=pltpu.SMEM)
CONTEXT_STEPS = (0, 4, 3, 7, 5, 2, 6, 1)
FIRST_KEYS = 256
MIB = 1024 * 1024


def place(index):
    return (index % W) * Z + index // W


def index_of(position):
    return (position % Z) * W + position // Z


def head_at(position):
    pos = lax.rem(position, RING)
    return lax.rem(pos, Z) * W + lax.div(pos, Z)


def blocks_by_head(y, seqs, mine):
    length = y.shape[0] // seqs
    for h in range(mine.shape[0]):
        mine[h] = jnp.concatenate(
            [y[r * length : (r + 1) * length, h * HEAD_DIM : (h + 1) * HEAD_DIM] for r in range(seqs)], axis=1
        ).astype(BF)


def keys_queries_kernel(pos_ref, gain_hbm, x_hbm, w_hbm, *refs):
    both, (normed, mine, gain_ref, x_ref, w_ref, gain_sem, x_sem, w_sem) = refs[:RING], refs[RING:]
    seqs, length, width = x_hbm.shape
    x_copies = [pltpu.make_async_copy(x_hbm.at[r], x_ref.at[r], x_sem.at[r]) for r in range(seqs)]
    w_copies = [pltpu.make_async_copy(w_hbm.at[c], w_ref.at[c], w_sem.at[c]) for c in range(2)]
    gain_copy = pltpu.make_async_copy(gain_hbm, gain_ref, gain_sem)
    for copy in (x_copies[0], gain_copy, *x_copies[1:], w_copies[1], w_copies[0]):
        copy.start()
    def norm(r):
        x = x_ref[r].astype(F32)
        mean = jnp.mean(x, axis=-1, keepdims=True)
        off = x - mean
        var = jnp.mean(off * off, axis=-1, keepdims=True)
        normed[r * length : (r + 1) * length] = (off / jnp.sqrt(var + 1e-05) * gain).astype(BF)

    def project(c, r):
        y = jnp.dot(normed[r * length : (r + 2) * length], w_ref[c], preferred_element_type=F32)
        for h in range(mine.shape[1]):
            columns = slice(h * HEAD_DIM, (h + 1) * HEAD_DIM)
            block = jnp.concatenate([y[:length, columns], y[length:, columns]], axis=1)
            mine[c, h, :, r * HEAD_DIM : (r + 2) * HEAD_DIM] = block.astype(BF)

    gain_copy.wait()
    gain = gain_ref[...].reshape(1, width)
    for r in range(seqs // 2):
        x_copies[r].wait()
        norm(r)
    for r in range(seqs // 2, seqs):
        x_copies[r].wait()
    w_copies[1].wait()
    for r in range(0, seqs // 2, 2):
        project(1, r)
    for r in range(seqs // 2, seqs):
        norm(r)
    w_copies[0].wait()
    for r in range(0, seqs // 2, 2):
        project(0, r)
    for r in range(seqs // 2, seqs, 2):
        project(1, r)
        project(0, r)
    pos = pos_ref[0]
    for c in (1, 0):
        for i, s in enumerate(STEPS):
            both[i][(1 - c) * length : (2 - c) * length] = mine[c, head_at(pos + s)]


def values_kernel(seqs, pos_ref, normed, w_hbm, *refs):
    outs, (mine, w_ref, w_sem) = refs[:RING], refs[RING:]
    copy = pltpu.make_async_copy(w_hbm.at[2], w_ref, w_sem)
    copy.start()
    copy.wait()
    blocks_by_head(jnp.dot(normed[...], w_ref[...], preferred_element_type=F32), seqs, mine)
    pos = pos_ref[0]
    for i, s in enumerate(STEPS):
        outs[i][...] = mine[head_at(pos + s)]


def put_by_sender(pos, parts, first, out):
    length = out.shape[2]
    for part, s in zip(parts, STEPS):
        src = lax.rem(pos + RING - s, RING)
        out[lax.div(src, Z), -s % Z] = part[first : first + length]


def place_kernel(count, pos_ref, *refs):
    put_by_sender(pos_ref[0], refs[:count], 0, refs[-1])


def half_terms(q, keys, side, out_hbm, terms, sem):
    half = keys.shape[1] * keys.shape[2]
    copies = []
    for i, (first, count) in enumerate(((0, FIRST_KEYS), (FIRST_KEYS, half - FIRST_KEYS))):
        total = None
        for w in range(W):
            term = lax.dot_general(
                q[w].reshape(half, -1),
                keys[w].reshape(half, -1)[first : first + count],
                (((1,), (1,)), ((), ())),
                preferred_element_type=F32,
            )
            total = term if total is None else total + term
        terms[:, first : first + count] = total.astype(BF)
        copies.append(
            pltpu.make_async_copy(
                terms.at[:, pl.ds(first, count)], out_hbm.at[:, pl.ds(side * half + first, count)], sem.at[i]
            )
        )
        copies[i].start()
    for copy in copies:
        copy.wait()


def near_kernel(pos_ref, *refs):
    parts, (k_ref, out_hbm, q, terms, sem) = refs[:RING], refs[RING:]
    put_by_sender(pos_ref[0], parts, q.shape[2], q)
    half_terms(q, k_ref, 0, out_hbm, terms, sem)


def far_kernel(_, q, k_far, out_hbm, terms, sem):
    half_terms(q, k_far, 1, out_hbm, terms, sem)


def probs_kernel(scale, x_ref, *refs):
    out_hbm, probs, sem = refs[-3:]
    logits = x_ref[0].astype(F32)
    for i in range(1, x_ref.shape[0]):
        logits = logits + x_ref[i].astype(F32)
    expo = jnp.exp(logits * scale)
    probs[...] = (expo / jnp.sum(expo, axis=-1, keepdims=True)).astype(BF)
    copies = [pltpu.make_async_copy(probs, out_hbm.at[i], sem.at[i]) for i in range(PLANE)]
    for copy in copies:
        copy.start()
    for copy in copies:
        copy.wait()


def seen_kernel(_, out_ref):
    out_ref[...] = jnp.zeros_like(out_ref)


def context_kernel(blocks, steps, pos_ref, p_ref, v_ref, v_far, _, *refs):
    outs, mine = refs[: len(steps)], refs[-1]
    half = v_ref.shape[1] * v_ref.shape[2]
    length = v_ref.shape[2]
    p = jnp.concatenate([p_ref[t * length : (t + 1) * length] for t in blocks], axis=0)
    for w in range(W):
        a = jnp.dot(p[:, :half], v_ref[w].reshape(half, -1), preferred_element_type=F32)
        a = a + jnp.dot(p[:, half:], v_far[w].reshape(half, -1), preferred_element_type=F32)
        mine[w] = a.astype(BF).reshape(mine.shape[1:])
    for out, s in zip(outs, steps):
        out[...] = mine[lax.div(lax.rem(pos_ref[0] + s, RING), Z), blocks.index(s % Z)]


def mix_kernel(pos_ref, w_ref, *refs):
    parts, (out_hbm, rows, mixed, sem) = refs[:RING], refs[RING:]
    pos = pos_ref[0]
    for i, s in enumerate(CONTEXT_STEPS):
        h = head_at(pos + RING - s)
        rows[i * HEAD_DIM : (i + 1) * HEAD_DIM] = w_ref[pl.ds(pl.multiple_of(h * HEAD_DIM, HEAD_DIM), HEAD_DIM)]
    copies = []
    for r in range(mixed.shape[0]):
        lhs = jnp.concatenate([part[:, r * HEAD_DIM : (r + 1) * HEAD_DIM] for part in parts], axis=1)
        mixed[r] = jnp.dot(lhs, rows[...], preferred_element_type=F32)
        copies.append(pltpu.make_async_copy(mixed.at[r], out_hbm.at[r], sem.at[r]))
        copies[r].start()
    for copy in copies:
        copy.wait()


def call(kernel, out_shape, operands, scratch=(), flops=0, hbm=(), unread=(), out_specs=None, aliases=None, vmem=20):
    moved = sum(math.prod(o.shape) * o.dtype.itemsize for o in operands)
    specs = [
        SMEM if o.dtype == jnp.int32 else HBM if i in hbm else ANY if i in unread else VMEM for i, o in enumerate(operands)
    ]
    return pl.pallas_call(
        kernel,
        out_shape=out_shape,
        in_specs=specs,
        out_specs=out_specs or jax.tree.map(lambda _: VMEM, out_shape),
        scratch_shapes=list(scratch),
        input_output_aliases=aliases or {},
        compiler_params=pltpu.CompilerParams(vmem_limit_bytes=vmem * MIB),
        cost_estimate=pl.CostEstimate(flops=flops, bytes_accessed=2 * moved, transcendentals=0),
    )(*operands)


def along_ring(parts, steps=STEPS):
    got = []
    for part, s in zip(parts, steps):
        pairs = [(i, index_of((place(i) + s) % RING)) for i in range(RING)]
        got.append(lax.ppermute(part, ("z", "w"), pairs) if s else part)
    return got


def other_core(a):
    return lax.ppermute(a, "c", [(0, 1), (1, 0)])


def shards(tokens, ln_gain, w_qkv, w_out):
    seqs, length, width = tokens.shape
    inner = w_qkv.shape[2]
    lanes = seqs * HEAD_DIM
    pos = (lax.axis_index("w") * Z + lax.axis_index("z")).astype(jnp.int32).reshape(1)
    pair = jax.ShapeDtypeStruct((2 * length, lanes), BF)
    block = jax.ShapeDtypeStruct((length, lanes), BF)
    whole = jax.ShapeDtypeStruct((W, Z, length, lanes), BF)
    half = Z * length
    full = CORE * half
    scale = 1.0 / math.sqrt(HEAD_DIM * seqs * W * PLANE)

    weights = jnp.transpose(w_qkv, (1, 0, 2))
    dma = pltpu.SemaphoreType.DMA
    *both, normed = call(
        keys_queries_kernel,
        [pair] * RING + [jax.ShapeDtypeStruct((seqs * length, width), BF)],
        [pos, ln_gain, tokens, weights],
        [
            pltpu.VMEM((2, RING, length, lanes), BF),
            pltpu.VMEM(ln_gain.shape, F32),
            pltpu.VMEM(tokens.shape, BF),
            pltpu.VMEM((2, width, inner), BF),
            dma,
            dma((seqs,)),
            dma((2,)),
        ],
        flops=2 * seqs * length * width * 2 * inner,
        hbm=(1, 2, 3),
        vmem=51,
    )
    both = along_ring(both)
    values = call(
        functools.partial(values_kernel, seqs),
        [block] * RING,
        [pos, normed, weights],
        [pltpu.VMEM((RING, length, lanes), BF), pltpu.VMEM((width, inner), BF), dma],
        flops=2 * seqs * length * width * inner,
        hbm=(2,),
        vmem=20,
    )
    keys = call(functools.partial(place_kernel, RING), whole, [pos, *both, values[0]], unread=(1 + RING,))
    keys_far = other_core(keys)
    values = along_ring(values)
    term, query = call(
        near_kernel,
        [jax.ShapeDtypeStruct((half, full), BF), whole],
        [pos, *both, keys],
        [pltpu.VMEM((half, half), BF), dma((2,))],
        flops=2 * half * half * W * lanes,
        out_specs=[HBM, VMEM],
    )
    term = call(
        far_kernel,
        jax.ShapeDtypeStruct((half, full), BF),
        [term, query, keys_far],
        [pltpu.VMEM((half, half), BF), dma((2,))],
        flops=2 * half * half * W * lanes,
        hbm=(0,),
        out_specs=HBM,
        aliases={0: 0},
    )
    chunk = (PLANE, half // PLANE, full)
    terms = lax.all_to_all(term.reshape(chunk), ("x", "y"), 0, 0, tiled=True)
    early = values[1:5]
    probs = call(
        functools.partial(probs_kernel, scale),
        jax.ShapeDtypeStruct(chunk, BF),
        [terms, *early],
        [pltpu.VMEM(chunk[1:], BF), dma((PLANE,))],
        unread=range(1, 5),
        out_specs=HBM,
    )
    probs = lax.all_to_all(probs, ("x", "y"), 0, 0, tiled=True).reshape(half, full)
    values = call(functools.partial(place_kernel, RING), whole, [pos, *values])
    values_far = other_core(values)
    seen = call(seen_kernel, jax.ShapeDtypeStruct((8, 128), F32), [values_far], unread=(0,))
    context = []
    for blocks in ((0, 3), (1, 2)):
        steps = [s for s in CONTEXT_STEPS if s % Z in blocks]
        parts = call(
            functools.partial(context_kernel, blocks, steps),
            [block] * len(steps),
            [pos, probs, values, values_far, seen],
            [pltpu.VMEM((W, len(blocks), length, lanes), BF)],
            flops=half * full * W * lanes,
            unread=(4,),
        )
        context += along_ring(parts, steps)
    return call(
        mix_kernel,
        jax.ShapeDtypeStruct((seqs, length, width), F32),
        [pos, w_out, *context],
        [pltpu.VMEM(w_out.shape, BF), pltpu.VMEM((seqs, length, width), F32), dma((seqs,))],
        flops=2 * seqs * length * inner * width,
        out_specs=HBM,
    )


def solution(mesh):
    cut = Mesh(mesh.devices.reshape(Z, CORE, X, Y, W), ("z", "c", "x", "y", "w"))
    split = P(("x", "y", "w"), ("z", "c"), None)
    return jax.shard_map(shards, mesh=cut, in_specs=(split, P(), P(), P()), out_specs=split, check_vma=False)
```

```python
import functools
import math

import jax
import jax.numpy as jnp
from jax import lax
from jax.experimental import pallas as pl
from jax.experimental.pallas import tpu as pltpu
from jax.sharding import Mesh
from jax.sharding import PartitionSpec as P

HEAD_DIM = 64
Z, CORE, X, Y, W = 4, 2, 4, 4, 2
RING = Z * W
PLANE = X * Y
STEPS = (0, 4, 3, 5, 2, 6, 1, 7)
BF = jnp.bfloat16
F32 = jnp.float32
VMEM = pl.BlockSpec(memory_space=pltpu.VMEM)
HBM = pl.BlockSpec(memory_space=pltpu.HBM)
ANY = pl.BlockSpec(memory_space=pl.ANY)
SMEM = pl.BlockSpec(memory_space=pltpu.SMEM)
CONTEXT_STEPS = (0, 4, 3, 7, 5, 2, 6, 1)
MIB = 1024 * 1024


def place(index):
    return (index % W) * Z + index // W


def index_of(position):
    return (position % Z) * W + position // Z


def head_at(position):
    pos = lax.rem(position, RING)
    return lax.rem(pos, Z) * W + lax.div(pos, Z)


def blocks_by_head(y, seqs, mine):
    length = y.shape[0] // seqs
    for h in range(mine.shape[0]):
        mine[h] = jnp.concatenate(
            [y[r * length : (r + 1) * length, h * HEAD_DIM : (h + 1) * HEAD_DIM] for r in range(seqs)], axis=1
        ).astype(BF)


def keys_queries_kernel(pos_ref, gain_hbm, x_hbm, w_hbm, *refs):
    both, (normed, mine, gain_ref, x_ref, w_ref, gain_sem, x_sem, w_sem) = refs[:RING], refs[RING:]
    seqs, length, width = x_hbm.shape
    x_copies = [pltpu.make_async_copy(x_hbm.at[r], x_ref.at[r], x_sem.at[r]) for r in range(seqs)]
    w_copies = [pltpu.make_async_copy(w_hbm.at[c], w_ref.at[c], w_sem.at[c]) for c in range(2)]
    gain_copy = pltpu.make_async_copy(gain_hbm, gain_ref, gain_sem)
    for copy in (x_copies[0], gain_copy, *x_copies[1:], w_copies[1], w_copies[0]):
        copy.start()
    def norm(r):
        x = x_ref[r].astype(F32)
        mean = jnp.mean(x, axis=-1, keepdims=True)
        off = x - mean
        var = jnp.mean(off * off, axis=-1, keepdims=True)
        normed[r * length : (r + 1) * length] = (off / jnp.sqrt(var + 1e-05) * gain).astype(BF)

    def project(c, r):
        y = jnp.dot(normed[r * length : (r + 2) * length], w_ref[c], preferred_element_type=F32).astype(BF)
        for h in range(mine.shape[1]):
            columns = slice(h * HEAD_DIM, (h + 1) * HEAD_DIM)
            block = jnp.concatenate([y[:length, columns], y[length:, columns]], axis=1)
            mine[c, h, :, r * HEAD_DIM : (r + 2) * HEAD_DIM] = block

    gain_copy.wait()
    gain = gain_ref[...].reshape(1, width)
    for r in range(seqs // 2):
        x_copies[r].wait()
        norm(r)
    for r in range(seqs // 2, seqs):
        x_copies[r].wait()
    w_copies[1].wait()
    for r in range(0, seqs // 2, 2):
        project(1, r)
    for r in range(seqs // 2, seqs):
        norm(r)
    w_copies[0].wait()
    for r in range(0, seqs // 2, 2):
        project(0, r)
    for r in range(seqs // 2, seqs, 2):
        project(1, r)
        project(0, r)
    pos = pos_ref[0]
    for c in (1, 0):
        for i, s in enumerate(STEPS):
            both[i][(1 - c) * length : (2 - c) * length] = mine[c, head_at(pos + s)]


def values_kernel(seqs, pos_ref, normed, w_hbm, *refs):
    outs, (mine, w_ref, w_sem) = refs[:RING], refs[RING:]
    copy = pltpu.make_async_copy(w_hbm.at[2], w_ref, w_sem)
    copy.start()
    copy.wait()
    blocks_by_head(jnp.dot(normed[...], w_ref[...], preferred_element_type=F32), seqs, mine)
    pos = pos_ref[0]
    for i, s in enumerate(STEPS):
        outs[i][...] = mine[head_at(pos + s)]


def cuts(rows, count):
    return [pl.ds(i * (rows // count), rows // count) for i in range(count)]


def put_by_sender(pos, parts, first, out):
    length = out.shape[2]
    for part, s in zip(parts, STEPS):
        src = lax.rem(pos + RING - s, RING)
        out[lax.div(src, Z), -s % Z] = part[first : first + length]


def place_kernel(count, pos_ref, *refs):
    put_by_sender(pos_ref[0], refs[:count], 0, refs[-1])


def half_terms(q, keys, side, out_hbm, terms, sem):
    length = keys.shape[2]
    half = keys.shape[1] * length
    columns = pl.ds(side * half, half)
    total = None
    for w in range(W):
        term = lax.dot_general(
            q[w].reshape(half, -1), keys[w].reshape(half, -1), (((1,), (1,)), ((), ())), preferred_element_type=F32
        )
        total = term if total is None else total + term
    copies = []
    for i, rows in enumerate(cuts(half, Z)):
        terms[rows] = total[i * length : (i + 1) * length].astype(BF)
        copies.append(pltpu.make_async_copy(terms.at[rows], out_hbm.at[rows, columns], sem.at[i]))
        copies[i].start()
    for copy in copies:
        copy.wait()


def near_kernel(pos_ref, *refs):
    parts, (k_ref, out_hbm, q, terms, sem) = refs[:RING], refs[RING:]
    put_by_sender(pos_ref[0], parts, q.shape[2], q)
    half_terms(q, k_ref, 0, out_hbm, terms, sem)


def far_kernel(_, q, k_far, out_hbm, terms, sem):
    half_terms(q, k_far, 1, out_hbm, terms, sem)


def probs_kernel(scale, x_ref, *refs):
    out_hbm, probs, sem = refs[-3:]
    logits = x_ref[0].astype(F32)
    for i in range(1, x_ref.shape[0]):
        logits = logits + x_ref[i].astype(F32)
    expo = jnp.exp(logits * scale)
    probs[...] = (expo / jnp.sum(expo, axis=-1, keepdims=True)).astype(BF)
    copies = [pltpu.make_async_copy(probs, out_hbm.at[i], sem.at[i]) for i in range(PLANE)]
    for copy in copies:
        copy.start()
    for copy in copies:
        copy.wait()


def seen_kernel(_, out_ref):
    out_ref[...] = jnp.zeros_like(out_ref)


def context_kernel(blocks, steps, pos_ref, p_ref, v_ref, v_far, _, *refs):
    outs, mine = refs[: len(steps)], refs[-1]
    half = v_ref.shape[1] * v_ref.shape[2]
    length = v_ref.shape[2]
    p = jnp.concatenate([p_ref[t * length : (t + 1) * length] for t in blocks], axis=0)
    for w in range(W):
        a = jnp.dot(p[:, :half], v_ref[w].reshape(half, -1), preferred_element_type=F32)
        a = a + jnp.dot(p[:, half:], v_far[w].reshape(half, -1), preferred_element_type=F32)
        mine[w] = a.astype(BF).reshape(mine.shape[1:])
    for out, s in zip(outs, steps):
        out[...] = mine[lax.div(lax.rem(pos_ref[0] + s, RING), Z), blocks.index(s % Z)]


def mix_kernel(pos_ref, w_ref, *refs):
    parts, (out_hbm, rows, mixed, sem) = refs[:RING], refs[RING:]
    pos = pos_ref[0]
    for i, s in enumerate(CONTEXT_STEPS):
        h = head_at(pos + RING - s)
        rows[i * HEAD_DIM : (i + 1) * HEAD_DIM] = w_ref[pl.ds(pl.multiple_of(h * HEAD_DIM, HEAD_DIM), HEAD_DIM)]
    copies = []
    for r in range(mixed.shape[0]):
        lhs = jnp.concatenate([part[:, r * HEAD_DIM : (r + 1) * HEAD_DIM] for part in parts], axis=1)
        mixed[r] = jnp.dot(lhs, rows[...], preferred_element_type=F32)
        copies.append(pltpu.make_async_copy(mixed.at[r], out_hbm.at[r], sem.at[r]))
        copies[r].start()
    for copy in copies:
        copy.wait()


def call(kernel, out_shape, operands, scratch=(), flops=0, hbm=(), unread=(), out_specs=None, aliases=None, vmem=20):
    moved = sum(math.prod(o.shape) * o.dtype.itemsize for o in operands)
    specs = [
        SMEM if o.dtype == jnp.int32 else HBM if i in hbm else ANY if i in unread else VMEM for i, o in enumerate(operands)
    ]
    return pl.pallas_call(
        kernel,
        out_shape=out_shape,
        in_specs=specs,
        out_specs=out_specs or jax.tree.map(lambda _: VMEM, out_shape),
        scratch_shapes=list(scratch),
        input_output_aliases=aliases or {},
        compiler_params=pltpu.CompilerParams(vmem_limit_bytes=vmem * MIB),
        cost_estimate=pl.CostEstimate(flops=flops, bytes_accessed=2 * moved, transcendentals=0),
    )(*operands)


def along_ring(parts, steps=STEPS):
    got = []
    for part, s in zip(parts, steps):
        pairs = [(i, index_of((place(i) + s) % RING)) for i in range(RING)]
        got.append(lax.ppermute(part, ("z", "w"), pairs) if s else part)
    return got


def other_core(a):
    return lax.ppermute(a, "c", [(0, 1), (1, 0)])


def shards(tokens, ln_gain, w_qkv, w_out):
    seqs, length, width = tokens.shape
    inner = w_qkv.shape[2]
    lanes = seqs * HEAD_DIM
    pos = (lax.axis_index("w") * Z + lax.axis_index("z")).astype(jnp.int32).reshape(1)
    pair = jax.ShapeDtypeStruct((2 * length, lanes), BF)
    block = jax.ShapeDtypeStruct((length, lanes), BF)
    whole = jax.ShapeDtypeStruct((W, Z, length, lanes), BF)
    half = Z * length
    full = CORE * half
    scale = 1.0 / math.sqrt(HEAD_DIM * seqs * W * PLANE)

    weights = jnp.transpose(w_qkv, (1, 0, 2))
    dma = pltpu.SemaphoreType.DMA
    *both, normed = call(
        keys_queries_kernel,
        [pair] * RING + [jax.ShapeDtypeStruct((seqs * length, width), BF)],
        [pos, ln_gain, tokens, weights],
        [
            pltpu.VMEM((2, RING, length, lanes), BF),
            pltpu.VMEM(ln_gain.shape, F32),
            pltpu.VMEM(tokens.shape, BF),
            pltpu.VMEM((2, width, inner), BF),
            dma,
            dma((seqs,)),
            dma((2,)),
        ],
        flops=2 * seqs * length * width * 2 * inner,
        hbm=(1, 2, 3),
        vmem=51,
    )
    both = along_ring(both)
    values = call(
        functools.partial(values_kernel, seqs),
        [block] * RING,
        [pos, normed, weights],
        [pltpu.VMEM((RING, length, lanes), BF), pltpu.VMEM((width, inner), BF), dma],
        flops=2 * seqs * length * width * inner,
        hbm=(2,),
        vmem=20,
    )
    keys = call(functools.partial(place_kernel, RING), whole, [pos, *both, values[0]], unread=(1 + RING,))
    keys_far = other_core(keys)
    values = along_ring(values)
    term, query = call(
        near_kernel,
        [jax.ShapeDtypeStruct((half, full), BF), whole],
        [pos, *both, keys],
        [pltpu.VMEM((half, half), BF), dma((Z,))],
        flops=2 * half * half * W * lanes,
        out_specs=[HBM, VMEM],
    )
    term = call(
        far_kernel,
        jax.ShapeDtypeStruct((half, full), BF),
        [term, query, keys_far],
        [pltpu.VMEM((half, half), BF), dma((Z,))],
        flops=2 * half * half * W * lanes,
        hbm=(0,),
        out_specs=HBM,
        aliases={0: 0},
    )
    chunk = (PLANE, half // PLANE, full)
    terms = lax.all_to_all(term.reshape(chunk), ("x", "y"), 0, 0, tiled=True)
    early = values[1:5]
    probs = call(
        functools.partial(probs_kernel, scale),
        jax.ShapeDtypeStruct(chunk, BF),
        [terms, *early],
        [pltpu.VMEM(chunk[1:], BF), dma((PLANE,))],
        unread=range(1, 5),
        out_specs=HBM,
    )
    probs = lax.all_to_all(probs, ("x", "y"), 0, 0, tiled=True).reshape(half, full)
    values = call(functools.partial(place_kernel, RING), whole, [pos, *values])
    values_far = other_core(values)
    seen = call(seen_kernel, jax.ShapeDtypeStruct((8, 128), F32), [values_far], unread=(0,))
    context = []
    for blocks in ((0, 3), (1, 2)):
        steps = [s for s in CONTEXT_STEPS if s % Z in blocks]
        parts = call(
            functools.partial(context_kernel, blocks, steps),
            [block] * len(steps),
            [pos, probs, values, values_far, seen],
            [pltpu.VMEM((W, len(blocks), length, lanes), BF)],
            flops=half * full * W * lanes,
            unread=(4,),
        )
        context += along_ring(parts, steps)
    return call(
        mix_kernel,
        jax.ShapeDtypeStruct((seqs, length, width), F32),
        [pos, w_out, *context],
        [pltpu.VMEM(w_out.shape, BF), pltpu.VMEM((seqs, length, width), F32), dma((seqs,))],
        flops=2 * seqs * length * inner * width,
        out_specs=HBM,
    )


def solution(mesh):
    cut = Mesh(mesh.devices.reshape(Z, CORE, X, Y, W), ("z", "c", "x", "y", "w"))
    split = P(("x", "y", "w"), ("z", "c"), None)
    return jax.shard_map(shards, mesh=cut, in_specs=(split, P(), P(), P()), out_specs=split, check_vma=False)
```

```python
import functools
import math

import jax
import jax.numpy as jnp
from jax import lax
from jax.experimental import pallas as pl
from jax.experimental.pallas import tpu as pltpu
from jax.sharding import Mesh
from jax.sharding import PartitionSpec as P

HEAD_DIM = 64
Z, CORE, X, Y, W = 4, 2, 4, 4, 2
RING = Z * W
PLANE = X * Y
STEPS = (0, 4, 3, 5, 2, 6, 1, 7)
BF = jnp.bfloat16
F32 = jnp.float32
VMEM = pl.BlockSpec(memory_space=pltpu.VMEM)
HBM = pl.BlockSpec(memory_space=pltpu.HBM)
ANY = pl.BlockSpec(memory_space=pl.ANY)
SMEM = pl.BlockSpec(memory_space=pltpu.SMEM)
CONTEXT_STEPS = (0, 4, 3, 7, 5, 2, 6, 1)
MIB = 1024 * 1024


def place(index):
    return (index % W) * Z + index // W


def index_of(position):
    return (position % Z) * W + position // Z


def head_at(position):
    pos = lax.rem(position, RING)
    return lax.rem(pos, Z) * W + lax.div(pos, Z)


def blocks_by_head(y, seqs, mine):
    length = y.shape[0] // seqs
    for h in range(mine.shape[0]):
        mine[h] = jnp.concatenate(
            [y[r * length : (r + 1) * length, h * HEAD_DIM : (h + 1) * HEAD_DIM] for r in range(seqs)], axis=1
        ).astype(BF)


def keys_queries_kernel(pos_ref, gain_hbm, x_hbm, w_hbm, *refs):
    both, (normed, mine, gain_ref, x_ref, w_ref, gain_sem, x_sem, w_sem) = refs[:RING], refs[RING:]
    seqs, length, width = x_hbm.shape
    x_copies = [pltpu.make_async_copy(x_hbm.at[r], x_ref.at[r], x_sem.at[r]) for r in range(seqs)]
    w_copies = [pltpu.make_async_copy(w_hbm.at[c], w_ref.at[c], w_sem.at[c]) for c in range(2)]
    gain_copy = pltpu.make_async_copy(gain_hbm, gain_ref, gain_sem)
    for copy in (x_copies[0], gain_copy, *x_copies[1:]):
        copy.start()
    def norm(r):
        x = x_ref[r].astype(F32)
        mean = jnp.mean(x, axis=-1, keepdims=True)
        off = x - mean
        var = jnp.mean(off * off, axis=-1, keepdims=True)
        normed[r * length : (r + 1) * length] = (off / jnp.sqrt(var + 1e-05) * gain).astype(BF)

    def project(c, r):
        y = jnp.dot(normed[r * length : (r + 2) * length], w_ref[c], preferred_element_type=F32).astype(BF)
        for h in range(mine.shape[1]):
            columns = slice(h * HEAD_DIM, (h + 1) * HEAD_DIM)
            block = jnp.concatenate([y[:length, columns], y[length:, columns]], axis=1)
            mine[c, h, :, r * HEAD_DIM : (r + 2) * HEAD_DIM] = block

    gain_copy.wait()
    gain = gain_ref[...].reshape(1, width)
    for r in range(seqs // 2):
        x_copies[r].wait()
    for c in (1, 0):
        w_copies[c].start()
    for r in range(seqs // 2):
        norm(r)
    for r in range(seqs // 2, seqs):
        x_copies[r].wait()
    w_copies[1].wait()
    for r in range(0, seqs // 2, 2):
        project(1, r)
    for r in range(seqs // 2, seqs):
        norm(r)
    w_copies[0].wait()
    for r in range(0, seqs // 2, 2):
        project(0, r)
    for r in range(seqs // 2, seqs, 2):
        project(1, r)
        project(0, r)
    pos = pos_ref[0]
    for c in (1, 0):
        for i, s in enumerate(STEPS):
            both[i][(1 - c) * length : (2 - c) * length] = mine[c, head_at(pos + s)]


def values_kernel(seqs, pos_ref, normed, w_hbm, *refs):
    outs, (mine, w_ref, w_sem) = refs[:RING], refs[RING:]
    copy = pltpu.make_async_copy(w_hbm.at[2], w_ref, w_sem)
    copy.start()
    copy.wait()
    blocks_by_head(jnp.dot(normed[...], w_ref[...], preferred_element_type=F32), seqs, mine)
    pos = pos_ref[0]
    for i, s in enumerate(STEPS):
        outs[i][...] = mine[head_at(pos + s)]


def cuts(rows, count):
    return [pl.ds(i * (rows // count), rows // count) for i in range(count)]


def put_by_sender(pos, parts, first, out):
    length = out.shape[2]
    for part, s in zip(parts, STEPS):
        src = lax.rem(pos + RING - s, RING)
        out[lax.div(src, Z), -s % Z] = part[first : first + length]


def place_kernel(count, pos_ref, *refs):
    put_by_sender(pos_ref[0], refs[:count], 0, refs[-1])


def half_terms(q, keys, side, out_hbm, terms, sem):
    length = keys.shape[2]
    half = keys.shape[1] * length
    columns = pl.ds(side * half, half)
    total = None
    for w in range(W):
        term = lax.dot_general(
            q[w].reshape(half, -1), keys[w].reshape(half, -1), (((1,), (1,)), ((), ())), preferred_element_type=F32
        )
        total = term if total is None else total + term
    copies = []
    for i, rows in enumerate(cuts(half, Z)):
        terms[rows] = total[i * length : (i + 1) * length].astype(BF)
        copies.append(pltpu.make_async_copy(terms.at[rows], out_hbm.at[rows, columns], sem.at[i]))
        copies[i].start()
    for copy in copies:
        copy.wait()


def near_kernel(pos_ref, *refs):
    parts, (k_ref, out_hbm, q, terms, sem) = refs[:RING], refs[RING:]
    put_by_sender(pos_ref[0], parts, q.shape[2], q)
    half_terms(q, k_ref, 0, out_hbm, terms, sem)


def far_kernel(_, q, k_far, out_hbm, terms, sem):
    half_terms(q, k_far, 1, out_hbm, terms, sem)


def probs_kernel(scale, x_ref, *refs):
    out_hbm, probs, sem = refs[-3:]
    logits = x_ref[0].astype(F32)
    for i in range(1, x_ref.shape[0]):
        logits = logits + x_ref[i].astype(F32)
    expo = jnp.exp(logits * scale)
    probs[...] = (expo / jnp.sum(expo, axis=-1, keepdims=True)).astype(BF)
    copies = [pltpu.make_async_copy(probs, out_hbm.at[i], sem.at[i]) for i in range(PLANE)]
    for copy in copies:
        copy.start()
    for copy in copies:
        copy.wait()


def seen_kernel(_, out_ref):
    out_ref[...] = jnp.zeros_like(out_ref)


def context_kernel(blocks, steps, pos_ref, p_ref, v_ref, v_far, _, *refs):
    outs, mine = refs[: len(steps)], refs[-1]
    half = v_ref.shape[1] * v_ref.shape[2]
    length = v_ref.shape[2]
    p = jnp.concatenate([p_ref[t * length : (t + 1) * length] for t in blocks], axis=0)
    for w in range(W):
        a = jnp.dot(p[:, :half], v_ref[w].reshape(half, -1), preferred_element_type=F32)
        a = a + jnp.dot(p[:, half:], v_far[w].reshape(half, -1), preferred_element_type=F32)
        mine[w] = a.astype(BF).reshape(mine.shape[1:])
    for out, s in zip(outs, steps):
        out[...] = mine[lax.div(lax.rem(pos_ref[0] + s, RING), Z), blocks.index(s % Z)]


def mix_kernel(pos_ref, w_ref, *refs):
    parts, (out_hbm, rows, mixed, sem) = refs[:RING], refs[RING:]
    pos = pos_ref[0]
    for i, s in enumerate(CONTEXT_STEPS):
        h = head_at(pos + RING - s)
        rows[i * HEAD_DIM : (i + 1) * HEAD_DIM] = w_ref[pl.ds(pl.multiple_of(h * HEAD_DIM, HEAD_DIM), HEAD_DIM)]
    copies = []
    for r in range(mixed.shape[0]):
        lhs = jnp.concatenate([part[:, r * HEAD_DIM : (r + 1) * HEAD_DIM] for part in parts], axis=1)
        mixed[r] = jnp.dot(lhs, rows[...], preferred_element_type=F32)
        copies.append(pltpu.make_async_copy(mixed.at[r], out_hbm.at[r], sem.at[r]))
        copies[r].start()
    for copy in copies:
        copy.wait()


def call(kernel, out_shape, operands, scratch=(), flops=0, hbm=(), unread=(), out_specs=None, aliases=None, vmem=20):
    moved = sum(math.prod(o.shape) * o.dtype.itemsize for o in operands)
    specs = [
        SMEM if o.dtype == jnp.int32 else HBM if i in hbm else ANY if i in unread else VMEM for i, o in enumerate(operands)
    ]
    return pl.pallas_call(
        kernel,
        out_shape=out_shape,
        in_specs=specs,
        out_specs=out_specs or jax.tree.map(lambda _: VMEM, out_shape),
        scratch_shapes=list(scratch),
        input_output_aliases=aliases or {},
        compiler_params=pltpu.CompilerParams(vmem_limit_bytes=vmem * MIB),
        cost_estimate=pl.CostEstimate(flops=flops, bytes_accessed=2 * moved, transcendentals=0),
    )(*operands)


def along_ring(parts, steps=STEPS):
    got = []
    for part, s in zip(parts, steps):
        pairs = [(i, index_of((place(i) + s) % RING)) for i in range(RING)]
        got.append(lax.ppermute(part, ("z", "w"), pairs) if s else part)
    return got


def other_core(a):
    return lax.ppermute(a, "c", [(0, 1), (1, 0)])


def shards(tokens, ln_gain, w_qkv, w_out):
    seqs, length, width = tokens.shape
    inner = w_qkv.shape[2]
    lanes = seqs * HEAD_DIM
    pos = (lax.axis_index("w") * Z + lax.axis_index("z")).astype(jnp.int32).reshape(1)
    pair = jax.ShapeDtypeStruct((2 * length, lanes), BF)
    block = jax.ShapeDtypeStruct((length, lanes), BF)
    whole = jax.ShapeDtypeStruct((W, Z, length, lanes), BF)
    half = Z * length
    full = CORE * half
    scale = 1.0 / math.sqrt(HEAD_DIM * seqs * W * PLANE)

    weights = jnp.transpose(w_qkv, (1, 0, 2))
    dma = pltpu.SemaphoreType.DMA
    *both, normed = call(
        keys_queries_kernel,
        [pair] * RING + [jax.ShapeDtypeStruct((seqs * length, width), BF)],
        [pos, ln_gain, tokens, weights],
        [
            pltpu.VMEM((2, RING, length, lanes), BF),
            pltpu.VMEM(ln_gain.shape, F32),
            pltpu.VMEM(tokens.shape, BF),
            pltpu.VMEM((2, width, inner), BF),
            dma,
            dma((seqs,)),
            dma((2,)),
        ],
        flops=2 * seqs * length * width * 2 * inner,
        hbm=(1, 2, 3),
        vmem=51,
    )
    both = along_ring(both)
    values = call(
        functools.partial(values_kernel, seqs),
        [block] * RING,
        [pos, normed, weights],
        [pltpu.VMEM((RING, length, lanes), BF), pltpu.VMEM((width, inner), BF), dma],
        flops=2 * seqs * length * width * inner,
        hbm=(2,),
        vmem=20,
    )
    keys = call(functools.partial(place_kernel, RING), whole, [pos, *both, values[0]], unread=(1 + RING,))
    keys_far = other_core(keys)
    values = along_ring(values)
    term, query = call(
        near_kernel,
        [jax.ShapeDtypeStruct((half, full), BF), whole],
        [pos, *both, keys],
        [pltpu.VMEM((half, half), BF), dma((Z,))],
        flops=2 * half * half * W * lanes,
        out_specs=[HBM, VMEM],
    )
    term = call(
        far_kernel,
        jax.ShapeDtypeStruct((half, full), BF),
        [term, query, keys_far],
        [pltpu.VMEM((half, half), BF), dma((Z,))],
        flops=2 * half * half * W * lanes,
        hbm=(0,),
        out_specs=HBM,
        aliases={0: 0},
    )
    chunk = (PLANE, half // PLANE, full)
    terms = lax.all_to_all(term.reshape(chunk), ("x", "y"), 0, 0, tiled=True)
    early = values[1:5]
    probs = call(
        functools.partial(probs_kernel, scale),
        jax.ShapeDtypeStruct(chunk, BF),
        [terms, *early],
        [pltpu.VMEM(chunk[1:], BF), dma((PLANE,))],
        unread=range(1, 5),
        out_specs=HBM,
    )
    probs = lax.all_to_all(probs, ("x", "y"), 0, 0, tiled=True).reshape(half, full)
    values = call(functools.partial(place_kernel, RING), whole, [pos, *values])
    values_far = other_core(values)
    seen = call(seen_kernel, jax.ShapeDtypeStruct((8, 128), F32), [values_far], unread=(0,))
    context = []
    for blocks in ((0, 3), (1, 2)):
        steps = [s for s in CONTEXT_STEPS if s % Z in blocks]
        parts = call(
            functools.partial(context_kernel, blocks, steps),
            [block] * len(steps),
            [pos, probs, values, values_far, seen],
            [pltpu.VMEM((W, len(blocks), length, lanes), BF)],
            flops=half * full * W * lanes,
            unread=(4,),
        )
        context += along_ring(parts, steps)
    return call(
        mix_kernel,
        jax.ShapeDtypeStruct((seqs, length, width), F32),
        [pos, w_out, *context],
        [pltpu.VMEM(w_out.shape, BF), pltpu.VMEM((seqs, length, width), F32), dma((seqs,))],
        flops=2 * seqs * length * inner * width,
        out_specs=HBM,
    )


def solution(mesh):
    cut = Mesh(mesh.devices.reshape(Z, CORE, X, Y, W), ("z", "c", "x", "y", "w"))
    split = P(("x", "y", "w"), ("z", "c"), None)
    return jax.shard_map(shards, mesh=cut, in_specs=(split, P(), P(), P()), out_specs=split, check_vma=False)
```

```python
import functools
import math

import jax
import jax.numpy as jnp
from jax import lax
from jax.experimental import pallas as pl
from jax.experimental.pallas import tpu as pltpu
from jax.sharding import Mesh
from jax.sharding import PartitionSpec as P

HEAD_DIM = 64
Z, CORE, X, Y, W = 4, 2, 4, 4, 2
RING = Z * W
PLANE = X * Y
STEPS = (0, 4, 3, 5, 2, 6, 1, 7)
BF = jnp.bfloat16
F32 = jnp.float32
VMEM = pl.BlockSpec(memory_space=pltpu.VMEM)
HBM = pl.BlockSpec(memory_space=pltpu.HBM)
ANY = pl.BlockSpec(memory_space=pl.ANY)
SMEM = pl.BlockSpec(memory_space=pltpu.SMEM)
CONTEXT_STEPS = (0, 4, 3, 7, 5, 2, 6, 1)
MIB = 1024 * 1024


def place(index):
    return (index % W) * Z + index // W


def index_of(position):
    return (position % Z) * W + position // Z


def head_at(position):
    pos = lax.rem(position, RING)
    return lax.rem(pos, Z) * W + lax.div(pos, Z)


def blocks_by_head(y, seqs, mine):
    length = y.shape[0] // seqs
    for h in range(mine.shape[0]):
        mine[h] = jnp.concatenate(
            [y[r * length : (r + 1) * length, h * HEAD_DIM : (h + 1) * HEAD_DIM] for r in range(seqs)], axis=1
        ).astype(BF)


def keys_queries_kernel(pos_ref, gain_hbm, x_hbm, w_hbm, *refs):
    both, (normed, mine, gain_ref, x_ref, w_ref, gain_sem, x_sem, w_sem) = refs[:RING], refs[RING:]
    seqs, length, width = x_hbm.shape
    x_copies = [pltpu.make_async_copy(x_hbm.at[r], x_ref.at[r], x_sem.at[r]) for r in range(seqs)]
    w_copies = [pltpu.make_async_copy(w_hbm.at[c], w_ref.at[c], w_sem.at[c]) for c in range(2)]
    gain_copy = pltpu.make_async_copy(gain_hbm, gain_ref, gain_sem)
    for copy in (x_copies[0], w_copies[1], gain_copy, *x_copies[1:], w_copies[0]):
        copy.start()
    def norm(r):
        x = x_ref[r].astype(F32)
        mean = jnp.mean(x, axis=-1, keepdims=True)
        off = x - mean
        var = jnp.mean(off * off, axis=-1, keepdims=True)
        normed[r * length : (r + 1) * length] = (off / jnp.sqrt(var + 1e-05) * gain).astype(BF)

    def project(c, r):
        y = jnp.dot(normed[r * length : (r + 2) * length], w_ref[c], preferred_element_type=F32).astype(BF)
        for h in range(mine.shape[1]):
            columns = slice(h * HEAD_DIM, (h + 1) * HEAD_DIM)
            block = jnp.concatenate([y[:length, columns], y[length:, columns]], axis=1)
            mine[c, h, :, r * HEAD_DIM : (r + 2) * HEAD_DIM] = block

    gain_copy.wait()
    gain = gain_ref[...].reshape(1, width)
    for r in range(seqs // 2):
        x_copies[r].wait()
        norm(r)
    for r in range(seqs // 2, seqs):
        x_copies[r].wait()
    w_copies[1].wait()
    for r in range(0, seqs // 2, 2):
        project(1, r)
    for r in range(seqs // 2, seqs):
        norm(r)
    for r in range(seqs // 2, seqs, 2):
        project(1, r)
    w_copies[0].wait()
    for r in range(0, seqs, 2):
        project(0, r)
    pos = pos_ref[0]
    for c in (1, 0):
        for i, s in enumerate(STEPS):
            both[i][(1 - c) * length : (2 - c) * length] = mine[c, head_at(pos + s)]


def values_kernel(seqs, pos_ref, normed, w_hbm, *refs):
    outs, (mine, w_ref, w_sem) = refs[:RING], refs[RING:]
    copy = pltpu.make_async_copy(w_hbm.at[2], w_ref, w_sem)
    copy.start()
    copy.wait()
    blocks_by_head(jnp.dot(normed[...], w_ref[...], preferred_element_type=F32), seqs, mine)
    pos = pos_ref[0]
    for i, s in enumerate(STEPS):
        outs[i][...] = mine[head_at(pos + s)]


def cuts(rows, count):
    return [pl.ds(i * (rows // count), rows // count) for i in range(count)]


def put_by_sender(pos, parts, first, out):
    length = out.shape[2]
    for part, s in zip(parts, STEPS):
        src = lax.rem(pos + RING - s, RING)
        out[lax.div(src, Z), -s % Z] = part[first : first + length]


def place_kernel(count, pos_ref, *refs):
    put_by_sender(pos_ref[0], refs[:count], 0, refs[-1])


def half_terms(q, keys, side, out_hbm, terms, sem):
    length = keys.shape[2]
    half = keys.shape[1] * length
    columns = pl.ds(side * half, half)
    total = None
    for w in range(W):
        term = lax.dot_general(
            q[w].reshape(half, -1), keys[w].reshape(half, -1), (((1,), (1,)), ((), ())), preferred_element_type=F32
        )
        total = term if total is None else total + term
    copies = []
    for i, rows in enumerate(cuts(half, Z)):
        terms[rows] = total[i * length : (i + 1) * length].astype(BF)
        copies.append(pltpu.make_async_copy(terms.at[rows], out_hbm.at[rows, columns], sem.at[i]))
        copies[i].start()
    for copy in copies:
        copy.wait()


def near_kernel(pos_ref, *refs):
    parts, (k_ref, out_hbm, q, terms, sem) = refs[:RING], refs[RING:]
    put_by_sender(pos_ref[0], parts, q.shape[2], q)
    half_terms(q, k_ref, 0, out_hbm, terms, sem)


def far_kernel(_, q, k_far, out_hbm, terms, sem):
    half_terms(q, k_far, 1, out_hbm, terms, sem)


def probs_kernel(scale, x_ref, *refs):
    out_hbm, probs, sem = refs[-3:]
    logits = x_ref[0].astype(F32)
    for i in range(1, x_ref.shape[0]):
        logits = logits + x_ref[i].astype(F32)
    expo = jnp.exp(logits * scale)
    probs[...] = (expo / jnp.sum(expo, axis=-1, keepdims=True)).astype(BF)
    copies = [pltpu.make_async_copy(probs, out_hbm.at[i], sem.at[i]) for i in range(PLANE)]
    for copy in copies:
        copy.start()
    for copy in copies:
        copy.wait()


def seen_kernel(_, out_ref):
    out_ref[...] = jnp.zeros_like(out_ref)


def context_kernel(blocks, steps, pos_ref, p_ref, v_ref, v_far, _, *refs):
    outs, mine = refs[: len(steps)], refs[-1]
    half = v_ref.shape[1] * v_ref.shape[2]
    length = v_ref.shape[2]
    p = jnp.concatenate([p_ref[t * length : (t + 1) * length] for t in blocks], axis=0)
    for w in range(W):
        a = jnp.dot(p[:, :half], v_ref[w].reshape(half, -1), preferred_element_type=F32)
        a = a + jnp.dot(p[:, half:], v_far[w].reshape(half, -1), preferred_element_type=F32)
        mine[w] = a.astype(BF).reshape(mine.shape[1:])
    for out, s in zip(outs, steps):
        out[...] = mine[lax.div(lax.rem(pos_ref[0] + s, RING), Z), blocks.index(s % Z)]


def mix_kernel(pos_ref, w_ref, *refs):
    parts, (out_hbm, rows, mixed, sem) = refs[:RING], refs[RING:]
    pos = pos_ref[0]
    for i, s in enumerate(CONTEXT_STEPS):
        h = head_at(pos + RING - s)
        rows[i * HEAD_DIM : (i + 1) * HEAD_DIM] = w_ref[pl.ds(pl.multiple_of(h * HEAD_DIM, HEAD_DIM), HEAD_DIM)]
    copies = []
    for r in range(mixed.shape[0]):
        lhs = jnp.concatenate([part[:, r * HEAD_DIM : (r + 1) * HEAD_DIM] for part in parts], axis=1)
        mixed[r] = jnp.dot(lhs, rows[...], preferred_element_type=F32)
        copies.append(pltpu.make_async_copy(mixed.at[r], out_hbm.at[r], sem.at[r]))
        copies[r].start()
    for copy in copies:
        copy.wait()


def call(kernel, out_shape, operands, scratch=(), flops=0, hbm=(), unread=(), out_specs=None, aliases=None, vmem=20):
    moved = sum(math.prod(o.shape) * o.dtype.itemsize for o in operands)
    specs = [
        SMEM if o.dtype == jnp.int32 else HBM if i in hbm else ANY if i in unread else VMEM for i, o in enumerate(operands)
    ]
    return pl.pallas_call(
        kernel,
        out_shape=out_shape,
        in_specs=specs,
        out_specs=out_specs or jax.tree.map(lambda _: VMEM, out_shape),
        scratch_shapes=list(scratch),
        input_output_aliases=aliases or {},
        compiler_params=pltpu.CompilerParams(vmem_limit_bytes=vmem * MIB),
        cost_estimate=pl.CostEstimate(flops=flops, bytes_accessed=2 * moved, transcendentals=0),
    )(*operands)


def along_ring(parts, steps=STEPS):
    got = []
    for part, s in zip(parts, steps):
        pairs = [(i, index_of((place(i) + s) % RING)) for i in range(RING)]
        got.append(lax.ppermute(part, ("z", "w"), pairs) if s else part)
    return got


def other_core(a):
    return lax.ppermute(a, "c", [(0, 1), (1, 0)])


def shards(tokens, ln_gain, w_qkv, w_out):
    seqs, length, width = tokens.shape
    inner = w_qkv.shape[2]
    lanes = seqs * HEAD_DIM
    pos = (lax.axis_index("w") * Z + lax.axis_index("z")).astype(jnp.int32).reshape(1)
    pair = jax.ShapeDtypeStruct((2 * length, lanes), BF)
    block = jax.ShapeDtypeStruct((length, lanes), BF)
    whole = jax.ShapeDtypeStruct((W, Z, length, lanes), BF)
    half = Z * length
    full = CORE * half
    scale = 1.0 / math.sqrt(HEAD_DIM * seqs * W * PLANE)

    weights = jnp.transpose(w_qkv, (1, 0, 2))
    dma = pltpu.SemaphoreType.DMA
    *both, normed = call(
        keys_queries_kernel,
        [pair] * RING + [jax.ShapeDtypeStruct((seqs * length, width), BF)],
        [pos, ln_gain, tokens, weights],
        [
            pltpu.VMEM((2, RING, length, lanes), BF),
            pltpu.VMEM(ln_gain.shape, F32),
            pltpu.VMEM(tokens.shape, BF),
            pltpu.VMEM((2, width, inner), BF),
            dma,
            dma((seqs,)),
            dma((2,)),
        ],
        flops=2 * seqs * length * width * 2 * inner,
        hbm=(1, 2, 3),
        vmem=51,
    )
    both = along_ring(both)
    values = call(
        functools.partial(values_kernel, seqs),
        [block] * RING,
        [pos, normed, weights],
        [pltpu.VMEM((RING, length, lanes), BF), pltpu.VMEM((width, inner), BF), dma],
        flops=2 * seqs * length * width * inner,
        hbm=(2,),
        vmem=20,
    )
    keys = call(functools.partial(place_kernel, RING), whole, [pos, *both, values[0]], unread=(1 + RING,))
    keys_far = other_core(keys)
    values = along_ring(values)
    term, query = call(
        near_kernel,
        [jax.ShapeDtypeStruct((half, full), BF), whole],
        [pos, *both, keys],
        [pltpu.VMEM((half, half), BF), dma((Z,))],
        flops=2 * half * half * W * lanes,
        out_specs=[HBM, VMEM],
    )
    term = call(
        far_kernel,
        jax.ShapeDtypeStruct((half, full), BF),
        [term, query, keys_far],
        [pltpu.VMEM((half, half), BF), dma((Z,))],
        flops=2 * half * half * W * lanes,
        hbm=(0,),
        out_specs=HBM,
        aliases={0: 0},
    )
    chunk = (PLANE, half // PLANE, full)
    terms = lax.all_to_all(term.reshape(chunk), ("x", "y"), 0, 0, tiled=True)
    early = values[1:5]
    probs = call(
        functools.partial(probs_kernel, scale),
        jax.ShapeDtypeStruct(chunk, BF),
        [terms, *early],
        [pltpu.VMEM(chunk[1:], BF), dma((PLANE,))],
        unread=range(1, 5),
        out_specs=HBM,
    )
    probs = lax.all_to_all(probs, ("x", "y"), 0, 0, tiled=True).reshape(half, full)
    values = call(functools.partial(place_kernel, RING), whole, [pos, *values])
    values_far = other_core(values)
    seen = call(seen_kernel, jax.ShapeDtypeStruct((8, 128), F32), [values_far], unread=(0,))
    context = []
    for blocks in ((0, 3), (1, 2)):
        steps = [s for s in CONTEXT_STEPS if s % Z in blocks]
        parts = call(
            functools.partial(context_kernel, blocks, steps),
            [block] * len(steps),
            [pos, probs, values, values_far, seen],
            [pltpu.VMEM((W, len(blocks), length, lanes), BF)],
            flops=half * full * W * lanes,
            unread=(4,),
        )
        context += along_ring(parts, steps)
    return call(
        mix_kernel,
        jax.ShapeDtypeStruct((seqs, length, width), F32),
        [pos, w_out, *context],
        [pltpu.VMEM(w_out.shape, BF), pltpu.VMEM((seqs, length, width), F32), dma((seqs,))],
        flops=2 * seqs * length * inner * width,
        out_specs=HBM,
    )


def solution(mesh):
    cut = Mesh(mesh.devices.reshape(Z, CORE, X, Y, W), ("z", "c", "x", "y", "w"))
    split = P(("x", "y", "w"), ("z", "c"), None)
    return jax.shard_map(shards, mesh=cut, in_specs=(split, P(), P(), P()), out_specs=split, check_vma=False)
```

```python
import functools
import math

import jax
import jax.numpy as jnp
from jax import lax
from jax.experimental import pallas as pl
from jax.experimental.pallas import tpu as pltpu
from jax.sharding import Mesh
from jax.sharding import PartitionSpec as P

HEAD_DIM = 64
Z, CORE, X, Y, W = 4, 2, 4, 4, 2
RING = Z * W
PLANE = X * Y
STEPS = (0, 4, 3, 5, 2, 6, 1, 7)
BF = jnp.bfloat16
F32 = jnp.float32
VMEM = pl.BlockSpec(memory_space=pltpu.VMEM)
HBM = pl.BlockSpec(memory_space=pltpu.HBM)
ANY = pl.BlockSpec(memory_space=pl.ANY)
SMEM = pl.BlockSpec(memory_space=pltpu.SMEM)
CONTEXT_STEPS = (0, 4, 2, 6, 3, 5, 1, 7)
MIB = 1024 * 1024


def place(index):
    return (index % W) * Z + index // W


def index_of(position):
    return (position % Z) * W + position // Z


def head_at(position):
    pos = lax.rem(position, RING)
    return lax.rem(pos, Z) * W + lax.div(pos, Z)


def blocks_by_head(y, seqs, mine):
    length = y.shape[0] // seqs
    for h in range(mine.shape[0]):
        mine[h] = jnp.concatenate(
            [y[r * length : (r + 1) * length, h * HEAD_DIM : (h + 1) * HEAD_DIM] for r in range(seqs)], axis=1
        ).astype(BF)


def keys_queries_kernel(pos_ref, gain_hbm, x_hbm, w_hbm, *refs):
    both, (normed, mine, gain_ref, x_ref, w_ref, gain_sem, x_sem, w_sem) = refs[:RING], refs[RING:]
    seqs, length, width = x_hbm.shape
    x_copies = [pltpu.make_async_copy(x_hbm.at[r], x_ref.at[r], x_sem.at[r]) for r in range(seqs)]
    w_copies = [pltpu.make_async_copy(w_hbm.at[c], w_ref.at[c], w_sem.at[c]) for c in range(2)]
    gain_copy = pltpu.make_async_copy(gain_hbm, gain_ref, gain_sem)
    for copy in (x_copies[0], gain_copy, *x_copies[1:], w_copies[1], w_copies[0]):
        copy.start()
    def norm(r):
        x = x_ref[r].astype(F32)
        mean = jnp.mean(x, axis=-1, keepdims=True)
        off = x - mean
        var = jnp.mean(off * off, axis=-1, keepdims=True)
        normed[r * length : (r + 1) * length] = (off / jnp.sqrt(var + 1e-05) * gain).astype(BF)

    def project(c, r):
        y = jnp.dot(normed[r * length : (r + 2) * length], w_ref[c], preferred_element_type=F32).astype(BF)
        for h in range(mine.shape[1]):
            columns = slice(h * HEAD_DIM, (h + 1) * HEAD_DIM)
            block = jnp.concatenate([y[:length, columns], y[length:, columns]], axis=1)
            mine[c, h, :, r * HEAD_DIM : (r + 2) * HEAD_DIM] = block

    gain_copy.wait()
    gain = gain_ref[...].reshape(1, width)
    for r in range(seqs // 2):
        x_copies[r].wait()
        norm(r)
    for r in range(seqs // 2, seqs):
        x_copies[r].wait()
    w_copies[1].wait()
    for r in range(0, seqs // 2, 2):
        project(1, r)
    for r in range(seqs // 2, seqs):
        norm(r)
    w_copies[0].wait()
    for r in range(0, seqs // 2, 2):
        project(0, r)
    for r in range(seqs // 2, seqs, 2):
        project(1, r)
        project(0, r)
    pos = pos_ref[0]
    for c in (1, 0):
        for i, s in enumerate(STEPS):
            both[i][(1 - c) * length : (2 - c) * length] = mine[c, head_at(pos + s)]


def values_kernel(seqs, pos_ref, normed, w_hbm, *refs):
    outs, (mine, w_ref, w_sem) = refs[:RING], refs[RING:]
    copy = pltpu.make_async_copy(w_hbm.at[2], w_ref, w_sem)
    copy.start()
    copy.wait()
    blocks_by_head(jnp.dot(normed[...], w_ref[...], preferred_element_type=F32), seqs, mine)
    pos = pos_ref[0]
    for i, s in enumerate(STEPS):
        outs[i][...] = mine[head_at(pos + s)]


def cuts(rows, count):
    return [pl.ds(i * (rows // count), rows // count) for i in range(count)]


def put_by_sender(pos, parts, first, out):
    length = out.shape[2]
    for part, s in zip(parts, STEPS):
        src = lax.rem(pos + RING - s, RING)
        out[lax.div(src, Z), -s % Z] = part[first : first + length]


def place_kernel(count, pos_ref, *refs):
    put_by_sender(pos_ref[0], refs[:count], 0, refs[-1])


def half_terms(q, keys, side, out_hbm, terms, sem):
    length = keys.shape[2]
    half = keys.shape[1] * length
    columns = pl.ds(side * half, half)
    total = None
    for w in range(W):
        term = lax.dot_general(
            q[w].reshape(half, -1), keys[w].reshape(half, -1), (((1,), (1,)), ((), ())), preferred_element_type=F32
        )
        total = term if total is None else total + term
    copies = []
    for i, rows in enumerate(cuts(half, Z)):
        terms[rows] = total[i * length : (i + 1) * length].astype(BF)
        copies.append(pltpu.make_async_copy(terms.at[rows], out_hbm.at[rows, columns], sem.at[i]))
        copies[i].start()
    for copy in copies:
        copy.wait()


def near_kernel(pos_ref, *refs):
    parts, (k_ref, out_hbm, q, terms, sem) = refs[:RING], refs[RING:]
    put_by_sender(pos_ref[0], parts, q.shape[2], q)
    half_terms(q, k_ref, 0, out_hbm, terms, sem)


def far_kernel(_, q, k_far, out_hbm, terms, sem):
    half_terms(q, k_far, 1, out_hbm, terms, sem)


def probs_kernel(scale, x_ref, *refs):
    out_hbm, probs, sem = refs[-3:]
    logits = x_ref[0].astype(F32)
    for i in range(1, x_ref.shape[0]):
        logits = logits + x_ref[i].astype(F32)
    expo = jnp.exp(logits * scale)
    probs[...] = (expo / jnp.sum(expo, axis=-1, keepdims=True)).astype(BF)
    copies = [pltpu.make_async_copy(probs, out_hbm.at[i], sem.at[i]) for i in range(PLANE)]
    for copy in copies:
        copy.start()
    for copy in copies:
        copy.wait()


def seen_kernel(_, out_ref):
    out_ref[...] = jnp.zeros_like(out_ref)


def context_kernel(blocks, steps, pos_ref, p_ref, v_ref, v_far, _, *refs):
    outs, mine = refs[: len(steps)], refs[-1]
    half = v_ref.shape[1] * v_ref.shape[2]
    length = v_ref.shape[2]
    p = jnp.concatenate([p_ref[t * length : (t + 1) * length] for t in blocks], axis=0)
    for w in range(W):
        a = jnp.dot(p[:, :half], v_ref[w].reshape(half, -1), preferred_element_type=F32)
        a = a + jnp.dot(p[:, half:], v_far[w].reshape(half, -1), preferred_element_type=F32)
        mine[w] = a.astype(BF).reshape(mine.shape[1:])
    for out, s in zip(outs, steps):
        out[...] = mine[lax.div(lax.rem(pos_ref[0] + s, RING), Z), blocks.index(s % Z)]


def mix_kernel(pos_ref, w_ref, *refs):
    parts, (out_hbm, rows, mixed, sem) = refs[:RING], refs[RING:]
    pos = pos_ref[0]
    for i, s in enumerate(CONTEXT_STEPS):
        h = head_at(pos + RING - s)
        rows[i * HEAD_DIM : (i + 1) * HEAD_DIM] = w_ref[pl.ds(pl.multiple_of(h * HEAD_DIM, HEAD_DIM), HEAD_DIM)]
    copies = []
    for r in range(mixed.shape[0]):
        lhs = jnp.concatenate([part[:, r * HEAD_DIM : (r + 1) * HEAD_DIM] for part in parts], axis=1)
        mixed[r] = jnp.dot(lhs, rows[...], preferred_element_type=F32)
        copies.append(pltpu.make_async_copy(mixed.at[r], out_hbm.at[r], sem.at[r]))
        copies[r].start()
    for copy in copies:
        copy.wait()


def call(kernel, out_shape, operands, scratch=(), flops=0, hbm=(), unread=(), out_specs=None, aliases=None, vmem=20):
    moved = sum(math.prod(o.shape) * o.dtype.itemsize for o in operands)
    specs = [
        SMEM if o.dtype == jnp.int32 else HBM if i in hbm else ANY if i in unread else VMEM for i, o in enumerate(operands)
    ]
    return pl.pallas_call(
        kernel,
        out_shape=out_shape,
        in_specs=specs,
        out_specs=out_specs or jax.tree.map(lambda _: VMEM, out_shape),
        scratch_shapes=list(scratch),
        input_output_aliases=aliases or {},
        compiler_params=pltpu.CompilerParams(vmem_limit_bytes=vmem * MIB),
        cost_estimate=pl.CostEstimate(flops=flops, bytes_accessed=2 * moved, transcendentals=0),
    )(*operands)


def along_ring(parts, steps=STEPS):
    got = []
    for part, s in zip(parts, steps):
        pairs = [(i, index_of((place(i) + s) % RING)) for i in range(RING)]
        got.append(lax.ppermute(part, ("z", "w"), pairs) if s else part)
    return got


def other_core(a):
    return lax.ppermute(a, "c", [(0, 1), (1, 0)])


def shards(tokens, ln_gain, w_qkv, w_out):
    seqs, length, width = tokens.shape
    inner = w_qkv.shape[2]
    lanes = seqs * HEAD_DIM
    pos = (lax.axis_index("w") * Z + lax.axis_index("z")).astype(jnp.int32).reshape(1)
    pair = jax.ShapeDtypeStruct((2 * length, lanes), BF)
    block = jax.ShapeDtypeStruct((length, lanes), BF)
    whole = jax.ShapeDtypeStruct((W, Z, length, lanes), BF)
    half = Z * length
    full = CORE * half
    scale = 1.0 / math.sqrt(HEAD_DIM * seqs * W * PLANE)

    weights = jnp.transpose(w_qkv, (1, 0, 2))
    dma = pltpu.SemaphoreType.DMA
    *both, normed = call(
        keys_queries_kernel,
        [pair] * RING + [jax.ShapeDtypeStruct((seqs * length, width), BF)],
        [pos, ln_gain, tokens, weights],
        [
            pltpu.VMEM((2, RING, length, lanes), BF),
            pltpu.VMEM(ln_gain.shape, F32),
            pltpu.VMEM(tokens.shape, BF),
            pltpu.VMEM((2, width, inner), BF),
            dma,
            dma((seqs,)),
            dma((2,)),
        ],
        flops=2 * seqs * length * width * 2 * inner,
        hbm=(1, 2, 3),
        vmem=51,
    )
    both = along_ring(both)
    values = call(
        functools.partial(values_kernel, seqs),
        [block] * RING,
        [pos, normed, weights],
        [pltpu.VMEM((RING, length, lanes), BF), pltpu.VMEM((width, inner), BF), dma],
        flops=2 * seqs * length * width * inner,
        hbm=(2,),
        vmem=20,
    )
    keys = call(functools.partial(place_kernel, RING), whole, [pos, *both, values[0]], unread=(1 + RING,))
    keys_far = other_core(keys)
    values = along_ring(values)
    term, query = call(
        near_kernel,
        [jax.ShapeDtypeStruct((half, full), BF), whole],
        [pos, *both, keys],
        [pltpu.VMEM((half, half), BF), dma((Z,))],
        flops=2 * half * half * W * lanes,
        out_specs=[HBM, VMEM],
    )
    term = call(
        far_kernel,
        jax.ShapeDtypeStruct((half, full), BF),
        [term, query, keys_far],
        [pltpu.VMEM((half, half), BF), dma((Z,))],
        flops=2 * half * half * W * lanes,
        hbm=(0,),
        out_specs=HBM,
        aliases={0: 0},
    )
    chunk = (PLANE, half // PLANE, full)
    terms = lax.all_to_all(term.reshape(chunk), ("x", "y"), 0, 0, tiled=True)
    early = values[1:5]
    probs = call(
        functools.partial(probs_kernel, scale),
        jax.ShapeDtypeStruct(chunk, BF),
        [terms, *early],
        [pltpu.VMEM(chunk[1:], BF), dma((PLANE,))],
        unread=range(1, 5),
        out_specs=HBM,
    )
    probs = lax.all_to_all(probs, ("x", "y"), 0, 0, tiled=True).reshape(half, full)
    values = call(functools.partial(place_kernel, RING), whole, [pos, *values])
    values_far = other_core(values)
    seen = call(seen_kernel, jax.ShapeDtypeStruct((8, 128), F32), [values_far], unread=(0,))
    context = []
    for blocks in ((0, 2), (1, 3)):
        steps = [s for s in CONTEXT_STEPS if s % Z in blocks]
        parts = call(
            functools.partial(context_kernel, blocks, steps),
            [block] * len(steps),
            [pos, probs, values, values_far, seen],
            [pltpu.VMEM((W, len(blocks), length, lanes), BF)],
            flops=half * full * W * lanes,
            unread=(4,),
        )
        context += along_ring(parts, steps)
    return call(
        mix_kernel,
        jax.ShapeDtypeStruct((seqs, length, width), F32),
        [pos, w_out, *context],
        [pltpu.VMEM(w_out.shape, BF), pltpu.VMEM((seqs, length, width), F32), dma((seqs,))],
        flops=2 * seqs * length * inner * width,
        out_specs=HBM,
    )


def solution(mesh):
    cut = Mesh(mesh.devices.reshape(Z, CORE, X, Y, W), ("z", "c", "x", "y", "w"))
    split = P(("x", "y", "w"), ("z", "c"), None)
    return jax.shard_map(shards, mesh=cut, in_specs=(split, P(), P(), P()), out_specs=split, check_vma=False)
```

```python
import functools
import math

import jax
import jax.numpy as jnp
from jax import lax
from jax.experimental import pallas as pl
from jax.experimental.pallas import tpu as pltpu
from jax.sharding import Mesh
from jax.sharding import PartitionSpec as P

HEAD_DIM = 64
Z, CORE, X, Y, W = 4, 2, 4, 4, 2
RING = Z * W
PLANE = X * Y
STEPS = (0, 4, 3, 5, 2, 6, 1, 7)
BF = jnp.bfloat16
F32 = jnp.float32
VMEM = pl.BlockSpec(memory_space=pltpu.VMEM)
HBM = pl.BlockSpec(memory_space=pltpu.HBM)
ANY = pl.BlockSpec(memory_space=pl.ANY)
SMEM = pl.BlockSpec(memory_space=pltpu.SMEM)
CONTEXT_STEPS = (0, 4, 3, 5, 2, 6, 1, 7)
MIB = 1024 * 1024


def place(index):
    return (index % W) * Z + index // W


def index_of(position):
    return (position % Z) * W + position // Z


def head_at(position):
    pos = lax.rem(position, RING)
    return lax.rem(pos, Z) * W + lax.div(pos, Z)


def blocks_by_head(y, seqs, mine):
    length = y.shape[0] // seqs
    for h in range(mine.shape[0]):
        mine[h] = jnp.concatenate(
            [y[r * length : (r + 1) * length, h * HEAD_DIM : (h + 1) * HEAD_DIM] for r in range(seqs)], axis=1
        ).astype(BF)


def keys_queries_kernel(pos_ref, gain_hbm, x_hbm, w_hbm, *refs):
    both, (normed, mine, gain_ref, x_ref, w_ref, gain_sem, x_sem, w_sem) = refs[:RING], refs[RING:]
    seqs, length, width = x_hbm.shape
    x_copies = [pltpu.make_async_copy(x_hbm.at[r], x_ref.at[r], x_sem.at[r]) for r in range(seqs)]
    w_copies = [pltpu.make_async_copy(w_hbm.at[c], w_ref.at[c], w_sem.at[c]) for c in range(2)]
    gain_copy = pltpu.make_async_copy(gain_hbm, gain_ref, gain_sem)
    for copy in (x_copies[0], gain_copy, *x_copies[1:], w_copies[1], w_copies[0]):
        copy.start()
    def norm(r):
        x = x_ref[r].astype(F32)
        mean = jnp.mean(x, axis=-1, keepdims=True)
        off = x - mean
        var = jnp.mean(off * off, axis=-1, keepdims=True)
        normed[r * length : (r + 1) * length] = (off / jnp.sqrt(var + 1e-05) * gain).astype(BF)

    def project(c, r):
        y = jnp.dot(normed[r * length : (r + 2) * length], w_ref[c], preferred_element_type=F32).astype(BF)
        for h in range(mine.shape[1]):
            columns = slice(h * HEAD_DIM, (h + 1) * HEAD_DIM)
            block = jnp.concatenate([y[:length, columns], y[length:, columns]], axis=1)
            mine[c, h, :, r * HEAD_DIM : (r + 2) * HEAD_DIM] = block

    gain_copy.wait()
    gain = gain_ref[...].reshape(1, width)
    for r in range(seqs // 2):
        x_copies[r].wait()
        norm(r)
    for r in range(seqs // 2, seqs):
        x_copies[r].wait()
    w_copies[1].wait()
    for r in range(0, seqs // 2, 2):
        project(1, r)
    for r in range(seqs // 2, seqs):
        norm(r)
    w_copies[0].wait()
    for r in range(0, seqs // 2, 2):
        project(0, r)
    for r in range(seqs // 2, seqs, 2):
        project(1, r)
        project(0, r)
    pos = pos_ref[0]
    for c in (1, 0):
        for i, s in enumerate(STEPS):
            both[i][(1 - c) * length : (2 - c) * length] = mine[c, head_at(pos + s)]


def values_kernel(seqs, pos_ref, normed, w_hbm, *refs):
    outs, (mine, w_ref, w_sem) = refs[:RING], refs[RING:]
    copy = pltpu.make_async_copy(w_hbm.at[2], w_ref, w_sem)
    copy.start()
    copy.wait()
    blocks_by_head(jnp.dot(normed[...], w_ref[...], preferred_element_type=F32), seqs, mine)
    pos = pos_ref[0]
    for i, s in enumerate(STEPS):
        outs[i][...] = mine[head_at(pos + s)]


def cuts(rows, count):
    return [pl.ds(i * (rows // count), rows // count) for i in range(count)]


def put_by_sender(pos, parts, first, out):
    length = out.shape[2]
    for part, s in zip(parts, STEPS):
        src = lax.rem(pos + RING - s, RING)
        out[lax.div(src, Z), -s % Z] = part[first : first + length]


def place_kernel(count, pos_ref, *refs):
    put_by_sender(pos_ref[0], refs[:count], 0, refs[-1])


def half_terms(q, keys, side, out_hbm, terms, sem):
    length = keys.shape[2]
    half = keys.shape[1] * length
    columns = pl.ds(side * half, half)
    total = None
    for w in range(W):
        term = lax.dot_general(
            q[w].reshape(half, -1), keys[w].reshape(half, -1), (((1,), (1,)), ((), ())), preferred_element_type=F32
        )
        total = term if total is None else total + term
    copies = []
    for i, rows in enumerate(cuts(half, Z)):
        terms[rows] = total[i * length : (i + 1) * length].astype(BF)
        copies.append(pltpu.make_async_copy(terms.at[rows], out_hbm.at[rows, columns], sem.at[i]))
        copies[i].start()
    for copy in copies:
        copy.wait()


def near_kernel(pos_ref, *refs):
    parts, (k_ref, out_hbm, q, terms, sem) = refs[:RING], refs[RING:]
    put_by_sender(pos_ref[0], parts, q.shape[2], q)
    half_terms(q, k_ref, 0, out_hbm, terms, sem)


def far_kernel(_, q, k_far, out_hbm, terms, sem):
    half_terms(q, k_far, 1, out_hbm, terms, sem)


def probs_kernel(scale, x_ref, *refs):
    out_hbm, probs, sem = refs[-3:]
    logits = x_ref[0].astype(F32)
    for i in range(1, x_ref.shape[0]):
        logits = logits + x_ref[i].astype(F32)
    expo = jnp.exp(logits * scale)
    probs[...] = (expo / jnp.sum(expo, axis=-1, keepdims=True)).astype(BF)
    copies = [pltpu.make_async_copy(probs, out_hbm.at[i], sem.at[i]) for i in range(PLANE)]
    for copy in copies:
        copy.start()
    for copy in copies:
        copy.wait()


def seen_kernel(_, out_ref):
    out_ref[...] = jnp.zeros_like(out_ref)


def context_kernel(blocks, steps, pos_ref, p_ref, v_ref, v_far, _, *refs):
    outs, mine = refs[: len(steps)], refs[-1]
    half = v_ref.shape[1] * v_ref.shape[2]
    length = v_ref.shape[2]
    p = jnp.concatenate([p_ref[t * length : (t + 1) * length] for t in blocks], axis=0)
    for w in range(W):
        a = jnp.dot(p[:, :half], v_ref[w].reshape(half, -1), preferred_element_type=F32)
        a = a + jnp.dot(p[:, half:], v_far[w].reshape(half, -1), preferred_element_type=F32)
        mine[w] = a.astype(BF).reshape(mine.shape[1:])
    for out, s in zip(outs, steps):
        out[...] = mine[lax.div(lax.rem(pos_ref[0] + s, RING), Z), blocks.index(s % Z)]


def mix_kernel(pos_ref, w_ref, *refs):
    parts, (out_hbm, rows, mixed, sem) = refs[:RING], refs[RING:]
    pos = pos_ref[0]
    for i, s in enumerate(CONTEXT_STEPS):
        h = head_at(pos + RING - s)
        rows[i * HEAD_DIM : (i + 1) * HEAD_DIM] = w_ref[pl.ds(pl.multiple_of(h * HEAD_DIM, HEAD_DIM), HEAD_DIM)]
    copies = []
    for r in range(mixed.shape[0]):
        lhs = jnp.concatenate([part[:, r * HEAD_DIM : (r + 1) * HEAD_DIM] for part in parts], axis=1)
        mixed[r] = jnp.dot(lhs, rows[...], preferred_element_type=F32)
        copies.append(pltpu.make_async_copy(mixed.at[r], out_hbm.at[r], sem.at[r]))
        copies[r].start()
    for copy in copies:
        copy.wait()


def call(kernel, out_shape, operands, scratch=(), flops=0, hbm=(), unread=(), out_specs=None, aliases=None, vmem=20):
    moved = sum(math.prod(o.shape) * o.dtype.itemsize for o in operands)
    specs = [
        SMEM if o.dtype == jnp.int32 else HBM if i in hbm else ANY if i in unread else VMEM for i, o in enumerate(operands)
    ]
    return pl.pallas_call(
        kernel,
        out_shape=out_shape,
        in_specs=specs,
        out_specs=out_specs or jax.tree.map(lambda _: VMEM, out_shape),
        scratch_shapes=list(scratch),
        input_output_aliases=aliases or {},
        compiler_params=pltpu.CompilerParams(vmem_limit_bytes=vmem * MIB),
        cost_estimate=pl.CostEstimate(flops=flops, bytes_accessed=2 * moved, transcendentals=0),
    )(*operands)


def along_ring(parts, steps=STEPS):
    got = []
    for part, s in zip(parts, steps):
        pairs = [(i, index_of((place(i) + s) % RING)) for i in range(RING)]
        got.append(lax.ppermute(part, ("z", "w"), pairs) if s else part)
    return got


def other_core(a):
    return lax.ppermute(a, "c", [(0, 1), (1, 0)])


def shards(tokens, ln_gain, w_qkv, w_out):
    seqs, length, width = tokens.shape
    inner = w_qkv.shape[2]
    lanes = seqs * HEAD_DIM
    pos = (lax.axis_index("w") * Z + lax.axis_index("z")).astype(jnp.int32).reshape(1)
    pair = jax.ShapeDtypeStruct((2 * length, lanes), BF)
    block = jax.ShapeDtypeStruct((length, lanes), BF)
    whole = jax.ShapeDtypeStruct((W, Z, length, lanes), BF)
    half = Z * length
    full = CORE * half
    scale = 1.0 / math.sqrt(HEAD_DIM * seqs * W * PLANE)

    weights = jnp.transpose(w_qkv, (1, 0, 2))
    dma = pltpu.SemaphoreType.DMA
    *both, normed = call(
        keys_queries_kernel,
        [pair] * RING + [jax.ShapeDtypeStruct((seqs * length, width), BF)],
        [pos, ln_gain, tokens, weights],
        [
            pltpu.VMEM((2, RING, length, lanes), BF),
            pltpu.VMEM(ln_gain.shape, F32),
            pltpu.VMEM(tokens.shape, BF),
            pltpu.VMEM((2, width, inner), BF),
            dma,
            dma((seqs,)),
            dma((2,)),
        ],
        flops=2 * seqs * length * width * 2 * inner,
        hbm=(1, 2, 3),
        vmem=51,
    )
    both = along_ring(both)
    values = call(
        functools.partial(values_kernel, seqs),
        [block] * RING,
        [pos, normed, weights],
        [pltpu.VMEM((RING, length, lanes), BF), pltpu.VMEM((width, inner), BF), dma],
        flops=2 * seqs * length * width * inner,
        hbm=(2,),
        vmem=20,
    )
    keys = call(functools.partial(place_kernel, RING), whole, [pos, *both, values[0]], unread=(1 + RING,))
    keys_far = other_core(keys)
    values = along_ring(values)
    term, query = call(
        near_kernel,
        [jax.ShapeDtypeStruct((half, full), BF), whole],
        [pos, *both, keys],
        [pltpu.VMEM((half, half), BF), dma((Z,))],
        flops=2 * half * half * W * lanes,
        out_specs=[HBM, VMEM],
    )
    term = call(
        far_kernel,
        jax.ShapeDtypeStruct((half, full), BF),
        [term, query, keys_far],
        [pltpu.VMEM((half, half), BF), dma((Z,))],
        flops=2 * half * half * W * lanes,
        hbm=(0,),
        out_specs=HBM,
        aliases={0: 0},
    )
    chunk = (PLANE, half // PLANE, full)
    terms = lax.all_to_all(term.reshape(chunk), ("x", "y"), 0, 0, tiled=True)
    early = values[1:5]
    probs = call(
        functools.partial(probs_kernel, scale),
        jax.ShapeDtypeStruct(chunk, BF),
        [terms, *early],
        [pltpu.VMEM(chunk[1:], BF), dma((PLANE,))],
        unread=range(1, 5),
        out_specs=HBM,
    )
    probs = lax.all_to_all(probs, ("x", "y"), 0, 0, tiled=True).reshape(half, full)
    values = call(functools.partial(place_kernel, RING), whole, [pos, *values])
    values_far = other_core(values)
    seen = call(seen_kernel, jax.ShapeDtypeStruct((8, 128), F32), [values_far], unread=(0,))
    context = []
    for blocks in ((0,), (1, 2, 3)):
        steps = [s for s in CONTEXT_STEPS if s % Z in blocks]
        parts = call(
            functools.partial(context_kernel, blocks, steps),
            [block] * len(steps),
            [pos, probs, values, values_far, seen],
            [pltpu.VMEM((W, len(blocks), length, lanes), BF)],
            flops=half * full * W * lanes,
            unread=(4,),
        )
        context += along_ring(parts, steps)
    return call(
        mix_kernel,
        jax.ShapeDtypeStruct((seqs, length, width), F32),
        [pos, w_out, *context],
        [pltpu.VMEM(w_out.shape, BF), pltpu.VMEM((seqs, length, width), F32), dma((seqs,))],
        flops=2 * seqs * length * inner * width,
        out_specs=HBM,
    )


def solution(mesh):
    cut = Mesh(mesh.devices.reshape(Z, CORE, X, Y, W), ("z", "c", "x", "y", "w"))
    split = P(("x", "y", "w"), ("z", "c"), None)
    return jax.shard_map(shards, mesh=cut, in_specs=(split, P(), P(), P()), out_specs=split, check_vma=False)
```
